128 devices in a mesh: dp: 16 (over y_hi, z, core), tp: 8 (over y_lo, x).
Axes of the slice: x: 4, y: 4 (y_hi: 2, y_lo: 2; y = y_hi * 2 + y_lo), z: 4, core: 2. Of those that a mesh axis runs over, the one named last changes fastest.
Arguments:
- hidden: bfloat16 [2, 64, 4096], P(None, 'dp'), may hold values from -500 to 500
- lengths: int32 [64], P('dp'), may hold values from 512 to 4096, as said below
- norm_gain: float32 [4096], replicated, may hold values from 0.1 to 1.9
- w_query: bfloat16 [4096, 4096], P(None, 'tp'), may hold values from -0.09375 to 0.09375
- key_weight_matrix: bfloat16 [4096, 1024], P(None, 'tp'), may hold values from -0.1875 to 0.1875
- value_weight_matrix: bfloat16 [4096, 1024], P(None, 'tp'), may hold values from -0.09375 to 0.09375
- w_out: bfloat16 [4096, 4096], P('tp'), may hold values from -0.75 to 0.75
- key_cache: bfloat16 [64, 8, 4096, 128], P('dp', 'tp'), may hold values from -1300 to 1300
- cached_value_rows: bfloat16 [64, 8, 4096, 128], P('dp', 'tp'), may hold values from -6 to 6
- next_query: bfloat16 [4096, 4096], P(('dp', 'tp')), may hold values from -0.09375 to 0.09375
- upcoming_key_weight: bfloat16 [1024, 4096], P(('dp', 'tp')), may hold values from -0.09375 to 0.09375
- upcoming_value_weight: bfloat16 [1024, 4096], P(('dp', 'tp')), may hold values from -0.09375 to 0.09375
Outputs:
- mixed: bfloat16 [2, 64, 4096], P(None, 'dp')
- next_query_tp: bfloat16 [4096, 4096], P('tp')
- next_key_tp: bfloat16 [1024, 4096], P('tp')
- next_value_tp: bfloat16 [1024, 4096], P('tp')
The draws below stay inside these ranges and needn't reach their ends.
Inputs may be any that keep to these rules, and one draw needn't show every extreme that they name: At least one row has all 4096 slots valid; the first lengths[r] slots of row r hold its context.
All inputs are finite; a program needn't handle non-finite values.
Results may differ from the reference program's by a relative error of at most 0.012.
The reference program's roundings to bfloat16 on the way count: a program that leaves them out, or rounds other values in their place, can miss the bound.
Values may be sent and summed in bfloat16 or wider, within the bound.
A program may use at most 192 MiB of HBM per device.

```python
import math
import jax
import jax.numpy as jnp
from jax import lax

MODEL_WIDTH = 4096
QUERY_HEADS = 32
KEY_VALUE_HEADS = 8
HEAD_WIDTH = 128
CONTEXT_SLOTS = 4096
DECODE_STEPS = 2
ROLLOUT_ROWS = 64


def draw_hidden(key, part):
    key = jax.random.fold_in(key, 11)
    base_key, row_key, column_key = jax.random.split(key, 3)
    base = jnp.clip(jax.random.normal(base_key, (DECODE_STEPS, ROLLOUT_ROWS, MODEL_WIDTH), jnp.float32), -5.0, 5.0)
    row_scale = jnp.exp(jax.random.uniform(row_key, (DECODE_STEPS, ROLLOUT_ROWS, 1), jnp.float32) * 2.302585)
    column_scale = jnp.exp(jax.random.uniform(column_key, (1, 1, MODEL_WIDTH), jnp.float32) * 2.302585)
    return (base * row_scale * column_scale).astype(jnp.bfloat16)


def draw_lengths(key, part):
    key = jax.random.fold_in(key, 23)
    length_key, top_key = jax.random.split(key)
    drawn = jax.random.randint(length_key, (ROLLOUT_ROWS,), CONTEXT_SLOTS // 8, CONTEXT_SLOTS + 1)
    chosen = jax.random.randint(top_key, (), 0, ROLLOUT_ROWS)
    return jnp.where(jnp.arange(ROLLOUT_ROWS) == chosen, CONTEXT_SLOTS, drawn).astype(jnp.int32)


def draw_key_cache(key, part):
    key = jax.random.fold_in(key, 37)
    base_key = jax.random.fold_in(key, 0)
    array_extent = (ROLLOUT_ROWS, KEY_VALUE_HEADS, CONTEXT_SLOTS, HEAD_WIDTH)
    base = 2.0 * jnp.clip(jax.random.normal(base_key, array_extent, jnp.float32), -6.0, 6.0)
    return base.astype(jnp.bfloat16)


def block_levels(stream_key, dims, cuts, low, largest):
    level = 1.0
    for axis_at, shards_of in cuts:
        steps = jax.random.uniform(jax.random.fold_in(jax.random.fold_in(stream_key, 6), axis_at), (shards_of,), jnp.float32, low / len(cuts), largest / len(cuts))
        level = level * jnp.repeat(jnp.exp(steps), dims[axis_at] // shards_of).reshape((-1,) + (1,) * (len(dims) - 1 - axis_at))
    return level


def normal_values(own_key, dims, width, most, cuts=(), kind=jnp.bfloat16):
    level = block_levels(own_key, dims, cuts, -0.22, 0.18) if cuts else 1.0
    values = jax.random.normal(own_key, dims, jnp.float32) * width * level
    return jnp.minimum(jnp.maximum(values, -most), most).astype(kind)


def setup_inputs(seed: int = 0) -> dict:
    seeds = jax.random.split(jax.random.key(seed), 13)
    hidden = draw_hidden(jax.random.fold_in(seeds[12], 71), 0)
    lengths = draw_lengths(jax.random.fold_in(seeds[12], 71), 0)
    norm_gain = jnp.clip(1.0 + 0.18 * jax.random.normal(seeds[2], (MODEL_WIDTH,), jnp.float32), 0.1, 1.9)
    w_query = normal_values(seeds[3], (MODEL_WIDTH, QUERY_HEADS * HEAD_WIDTH), MODEL_WIDTH ** -0.5, 0.09375, ((1, 8),))
    key_weight_matrix = normal_values(seeds[4], (MODEL_WIDTH, KEY_VALUE_HEADS * HEAD_WIDTH), (MODEL_WIDTH // 4) ** -0.5, 0.1875, ((1, 8),))
    value_weight_matrix = normal_values(seeds[5], (MODEL_WIDTH, KEY_VALUE_HEADS * HEAD_WIDTH), MODEL_WIDTH ** -0.5, 0.09375, ((1, 8),))
    w_out = normal_values(seeds[6], (QUERY_HEADS * HEAD_WIDTH, MODEL_WIDTH), (QUERY_HEADS * HEAD_WIDTH // 64) ** -0.5, 0.75, ((0, 8),))
    key_cache = draw_key_cache(jax.random.fold_in(seeds[12], 71), 0)
    cached_value_rows = normal_values(seeds[8], (ROLLOUT_ROWS, KEY_VALUE_HEADS, CONTEXT_SLOTS, HEAD_WIDTH), 1.0, 6.0, ((0, 16), (1, 8)))
    next_query = normal_values(seeds[9], (QUERY_HEADS * HEAD_WIDTH, MODEL_WIDTH), MODEL_WIDTH ** -0.5, 0.09375, ((0, 128),))
    upcoming_key_weight = normal_values(seeds[10], (KEY_VALUE_HEADS * HEAD_WIDTH, MODEL_WIDTH), MODEL_WIDTH ** -0.5, 0.09375, ((0, 128),))
    upcoming_value_weight = normal_values(seeds[11], (KEY_VALUE_HEADS * HEAD_WIDTH, MODEL_WIDTH), MODEL_WIDTH ** -0.5, 0.09375, ((0, 128),))
    return {"hidden": hidden, "lengths": lengths, "norm_gain": norm_gain, "w_query": w_query, "key_weight_matrix": key_weight_matrix, "value_weight_matrix": value_weight_matrix, "w_out": w_out, "key_cache": key_cache, "cached_value_rows": cached_value_rows, "next_query": next_query, "upcoming_key_weight": upcoming_key_weight, "upcoming_value_weight": upcoming_value_weight}


def normalize(rows_in, gain):
    values = rows_in.astype(jnp.float32)
    scale = lax.rsqrt(lax.optimization_barrier(jnp.mean(values * values, axis=-1, keepdims=True)) + 1e-06)
    return (values * scale * gain.astype(jnp.float32)).astype(jnp.bfloat16)

def apply_rotation(vectors, token_positions):
    head_size = vectors.shape[-1]
    midpoint = head_size // 2
    frequency = jnp.power(1000000.0, -jnp.arange(midpoint, dtype=jnp.float32) * 2.0 / head_size)
    angles = token_positions.astype(jnp.float32)[:, None] * frequency[None, :]
    cosine = jnp.concatenate([jnp.cos(angles), jnp.cos(angles)], axis=-1)[:, None, :]
    sine_part = jnp.concatenate([jnp.sin(angles), jnp.sin(angles)], axis=-1)[:, None, :]
    leading = vectors[..., :midpoint]
    trailing = vectors[..., midpoint:]
    turned = jnp.concatenate([-trailing, leading], axis=-1)
    return vectors * cosine + turned * sine_part

def attend_row(pieces):
    query_rows, current_key_rows, current_value_rows, keys, values, length = pieces
    step_count = query_rows.shape[0]
    context = keys.shape[1]
    scale = 1.0 / math.sqrt(query_rows.shape[-1])
    query_wide = query_rows.astype(jnp.float32)
    cached = jnp.einsum('sgqd,gkd->sgqk', query_wide, keys.astype(jnp.float32)) * scale
    valid = (jnp.arange(context) < length)[None, None, None, :]
    cached = jnp.where(valid, cached, -jnp.inf)
    recent = jnp.einsum('sgqd,tgd->sgqt', query_wide, current_key_rows.astype(jnp.float32)) * scale
    causal = (jnp.arange(step_count)[None, :] <= jnp.arange(step_count)[:, None])[:, None, None, :]
    recent = jnp.where(causal, recent, -jnp.inf)
    top = jnp.maximum(lax.optimization_barrier(jnp.max(cached, axis=-1, keepdims=True)), lax.optimization_barrier(jnp.max(recent, axis=-1, keepdims=True)))
    cached_exp = jnp.exp(cached - top)
    recent_exp = jnp.exp(recent - top)
    total = lax.optimization_barrier(jnp.sum(cached_exp, axis=-1, keepdims=True)) + lax.optimization_barrier(jnp.sum(recent_exp, axis=-1, keepdims=True))
    cached_weight = (cached_exp / total).astype(jnp.bfloat16)
    recent_weight = (recent_exp / total).astype(jnp.bfloat16)
    result = jnp.einsum('sgqk,gkd->sgqd', cached_weight.astype(jnp.float32), values.astype(jnp.float32))
    result = result + jnp.einsum('sgqt,tgd->sgqd', recent_weight.astype(jnp.float32), current_value_rows.astype(jnp.float32))
    return result.astype(jnp.bfloat16)

def reference(hidden, lengths, norm_gain, w_query, key_weight_matrix, value_weight_matrix, w_out, key_cache, cached_value_rows, next_query, upcoming_key_weight, upcoming_value_weight):
    flat = hidden.reshape(DECODE_STEPS * ROLLOUT_ROWS, MODEL_WIDTH)
    normalized_input = normalize(flat, norm_gain)
    token_positions = jnp.concatenate([lengths + step for step in range(DECODE_STEPS)]).astype(jnp.int32)
    query_rows = jnp.dot(normalized_input, w_query, preferred_element_type=jnp.float32).reshape(DECODE_STEPS * ROLLOUT_ROWS, QUERY_HEADS, HEAD_WIDTH)
    query_rows = apply_rotation(query_rows, token_positions).astype(jnp.bfloat16).reshape(DECODE_STEPS, ROLLOUT_ROWS, KEY_VALUE_HEADS, QUERY_HEADS // KEY_VALUE_HEADS, HEAD_WIDTH)
    current_key_rows = jnp.dot(normalized_input, key_weight_matrix, preferred_element_type=jnp.float32).reshape(DECODE_STEPS * ROLLOUT_ROWS, KEY_VALUE_HEADS, HEAD_WIDTH)
    current_key_rows = apply_rotation(current_key_rows, token_positions).astype(jnp.bfloat16).reshape(DECODE_STEPS, ROLLOUT_ROWS, KEY_VALUE_HEADS, HEAD_WIDTH)
    current_value_rows = jnp.dot(normalized_input, value_weight_matrix, preferred_element_type=jnp.float32).astype(jnp.bfloat16)
    current_value_rows = current_value_rows.reshape(DECODE_STEPS, ROLLOUT_ROWS, KEY_VALUE_HEADS, HEAD_WIDTH)
    attended = lax.map(attend_row, (jnp.swapaxes(query_rows, 0, 1), jnp.swapaxes(current_key_rows, 0, 1), jnp.swapaxes(current_value_rows, 0, 1), key_cache, cached_value_rows, lengths))
    attended = jnp.swapaxes(attended, 0, 1).reshape(DECODE_STEPS * ROLLOUT_ROWS, QUERY_HEADS * HEAD_WIDTH)
    mixed = jnp.dot(attended, w_out, preferred_element_type=jnp.float32).astype(jnp.bfloat16)
    return (mixed.reshape(DECODE_STEPS, ROLLOUT_ROWS, MODEL_WIDTH), next_query, upcoming_key_weight, upcoming_value_weight)
```

```python
import functools
import math

import jax
import jax.numpy as jnp
from jax import lax
from jax.experimental import pallas as pl
from jax.experimental.pallas import tpu as pltpu
from jax.sharding import PartitionSpec as P

MESH = pl.DeviceIdType.MESH
BF = jnp.bfloat16
F32 = jnp.float32

CROSS = 1024
CROSS_PARTS = 2
TURN_PARTS = 6
VMEM_LIMIT = 36 * 2**20
ORDER = (
    0, 18, 9, 24, 1, 54, 55, 2, 19, 30, 56, 10, 11, 25, 36, 57, 3, 4, 58, 59, 5, 20, 60, 61, 62, 31, 42, 63,
    12, 13, 64, 14, 26, 65, 66, 37, 48, 67, 6, 21, 68, 69, 70, 32, 71, 72, 43, 15, 73, 27, 74, 75, 38, 76,
    77, 49, 7, 22, 33, 44, 16, 28, 39, 78, 50, 34, 45, 40, 51, 79, 46, 52, 8, 23, 17, 29, 35, 41, 47, 53,
)


def place():
    dp, tp = lax.axis_index("dp"), lax.axis_index("tp")
    return tp % 4, (dp // 8) * 2 + tp // 4, (dp // 2) % 4, dp % 2


def device(x, y, z, core):
    return ((y // 2) * 8 + z * 2 + core, (y % 2) * 4 + x)


def cut(start, width, parts):
    tiles = width // 128
    edges = [128 * (tiles * i // parts) for i in range(parts + 1)]
    return [(start + edges[i], edges[i + 1] - edges[i]) for i in range(parts)]


class Gather:
    def __init__(self, rows, width):
        self.rows, self.width = rows, width
        cuts = cut(0, CROSS, CROSS_PARTS) + cut(CROSS, width - CROSS, TURN_PARTS)
        self.parts = [(n < CROSS_PARTS, at, size) for n, (at, size) in enumerate(cuts)]
        self.count = len(cuts) * 10

    def scratch(self):
        return [
            pltpu.VMEM((2, self.rows, self.width), BF),
            pltpu.VMEM((4, 2, self.rows, CROSS), BF),
            pltpu.SemaphoreType.DMA((self.count,)),
            pltpu.SemaphoreType.DMA((self.count,)),
        ]

    def begin(self, held, moved, ring, sent, got):
        self.held, self.moved, self.ring, self.sent, self.got = held, moved, ring, sent, got
        self.x, self.y, self.z, self.core = place()
        self.ends = []

    def greetings(self):
        x, y, z, core = self.x, self.y, self.z, self.core
        senders = [device(x, y, (z + i) % 4, core) for i in range(1, 4)]
        senders += [device((x + i) % 4, y, z, core) for i in range(1, 4)]
        senders += [device(x, y, z, 1 - core)]
        near = [device((x + i) % 4, y % 2 * 2 + j, z, core) for i in range(4) for j in range(2)]
        edge = (y == 0) | (y == 3)
        return senders, near, edge

    def send(self, source, target, sent, got, to, when=None):
        copy = pltpu.make_async_remote_copy(
            src_ref=source,
            dst_ref=target,
            send_sem=self.sent.at[sent],
            recv_sem=self.got.at[got],
            device_id=to,
            device_id_type=MESH,
        )
        if when is None:
            copy.start()
            self.ends.append(copy.wait_send)
        else:
            pl.when(when)(copy.start)
            self.ends.append(lambda: pl.when(when)(copy.wait_send))

    def arrive(self, target, got):
        pltpu.make_async_remote_copy(
            src_ref=target,
            dst_ref=target,
            send_sem=self.sent.at[0],
            recv_sem=self.got.at[got],
            device_id=device(self.x, self.y, self.z, 1 - self.core),
            device_id_type=MESH,
        ).wait_recv()

    def z_start(self, view, sent, got):
        own = view(0)
        self.send(own, own, sent, got, device(self.x, self.y, (self.z + 1) % 4, self.core))
        self.send(own, own, sent + 1, got + 1, device(self.x, self.y, (self.z + 3) % 4, self.core))

    def z_pass(self, view, sent, got, upward):
        near, step = (3, 1) if upward else (1, 3)
        piece = view(near)
        self.arrive(piece, got + (0 if upward else 1))
        self.send(piece, piece, sent + 2, got + 2, device(self.x, self.y, (self.z + step) % 4, self.core))

    def z_other(self, view, got, upward):
        self.arrive(view(1 if upward else 3), got + (1 if upward else 0))

    def z_far(self, view, got):
        self.arrive(view(2), got + 2)

    def both(self, view, target, sent, got, x, stays):
        y = self.y
        for which in range(2):
            goal_y = y // 2 + 2 * which
            here = stays & (goal_y == y)
            self.send(view, target, sent + which, got + y % 2, device(x, goal_y, self.z, self.core), jnp.logical_not(here))
            pl.when(here)(pltpu.make_async_copy(view, target, self.sent.at[sent + which]).start)

    def land(self, view, target, slot, sent, got, stays):
        y = self.y
        here = stays & (y % 2 * 2 + slot == y)
        pl.when(here)(pltpu.make_async_copy(view, target, self.sent.at[sent + y // 2]).wait)
        pl.when(jnp.logical_not(here))(lambda: self.arrive(target, got + slot))

    def share(self, whole, sem):
        self.send(whole(self.core), whole(self.core), sem, sem, device(self.x, self.y, self.z, 1 - self.core))

    def cross_steps(self, n):
        at, size = self.parts[n][1:]
        base = n * 10
        upward = n % 2 == 0
        x, y, z, core = self.x, self.y, self.z, self.core
        columns, slots = pl.ds(at, size), pl.ds(0, 2)
        here = jnp.bool_(True)
        first = self.moved.at[0, :, columns]
        view = lambda step: self.ring.at[(z + step) % 4, :, :, columns]
        at_z = lambda to_x: self.ring.at[to_x, :, :, columns]
        final = lambda from_x: self.held.at[core, slots, from_x, :, columns]
        whole = lambda core: self.held.at[core, slots, :, :, columns]

        def start():
            self.both(first, self.ring.at[z, y % 2, :, columns], base, base, x, here)

        def column():
            for slot in range(2):
                self.land(first, self.ring.at[z, slot, :, columns], slot, base, base, here)
            self.z_start(view, base + 2, base + 2)

        def cross(step):
            goal = (z + step) % 4
            hops = (goal - x + 4) % 4
            to = device(goal, y, z, core)
            self.send(at_z(goal), final(x), base + 5 + step, base + 4 + hops, to, hops != 0)
            stay = pltpu.make_async_copy(at_z(goal), final(x), self.sent.at[base + 5 + step])
            pl.when(hops == 0)(stay.start)

        def relay():
            self.z_pass(view, base + 2, base + 2, upward)

        def second():
            self.z_other(view, base + 2, upward)
            cross(1 if upward else 3)

        def far():
            self.z_far(view, base + 2)
            cross(2)

        def finish():
            step = (x - z + 4) % 4
            pltpu.make_async_copy(at_z(x), final(x), self.sent.at[base + 5 + step]).wait()
            for hops in range(1, 4):
                self.arrive(final((x + 4 - hops) % 4), base + 4 + hops)
            self.share(whole, base + 9)

        def done():
            self.arrive(whole(1 - core), base + 9)

        return [
            ("start", start),
            ("column", column),
            ("cross0", functools.partial(cross, 0)),
            ("relay", relay),
            ("cross1", functools.partial(cross, 3 if upward else 1)),
            ("second", second),
            ("far", far),
            ("finish", finish),
            ("done", done),
        ]

    def turn_steps(self, n):
        at, size = self.parts[n][1:]
        base = n * 10
        upward = n % 2 == 0
        x, y, z, core = self.x, self.y, self.z, self.core
        columns, slots = pl.ds(at, size), pl.ds(0, 2)
        shift = (x + n) % 4
        goal = (z + 8 - x - n % 4) % 4
        at_x = lambda step: (z + step + 8 - x - n % 4) % 4
        pair = lambda step: self.held.at[core, slots, at_x(step), :, columns]
        whole = lambda core: self.held.at[core, slots, :, :, columns]
        first, shifted = (self.moved.at[slot, :, columns] for slot in range(2))
        view = self.moved.at[jnp.where(shift == 0, 0, 1), :, columns]

        def start():
            self.send(first, shifted, base, base, device(x, y, (z + shift) % 4, core), shift != 0)

        def turn():
            pl.when(shift != 0)(lambda: self.arrive(shifted, base))
            self.both(view, self.held.at[core, y % 2, x, :, columns], base + 1, base + 1, goal, goal == x)

        def column():
            for slot in range(2):
                target = self.held.at[core, slot, at_x(0), :, columns]
                self.land(view, target, slot, base + 1, base + 1, at_x(0) == x)
            self.z_start(pair, base + 3, base + 3)

        def relay():
            self.z_pass(pair, base + 3, base + 3, upward)

        def finish():
            self.z_other(pair, base + 3, upward)
            self.z_far(pair, base + 3)
            self.share(whole, base + 9)

        def done():
            self.arrive(whole(1 - core), base + 9)

        return [
            ("start", start),
            ("turn", turn),
            ("column", column),
            ("relay", relay),
            ("finish", finish),
            ("done", done),
        ]

    def steps(self):
        steps = {}
        for n, part in enumerate(self.parts):
            made = self.cross_steps(n) if part[0] else self.turn_steps(n)
            steps.update({f"{n}.{name}": step for name, step in made})
        return steps

    def finish(self):
        for end in self.ends:
            end()


def greet(senders, near, edge, loads):
    barrier = pltpu.get_barrier_semaphore()
    me = (lax.axis_index("dp"), lax.axis_index("tp"))
    signal = lambda peer: pl.semaphore_signal(barrier, inc=1, device_id=peer, device_id_type=MESH)
    for peer in senders:
        signal(peer)
    for peer in near:
        pl.when((peer[0] != me[0]) | (peer[1] != me[1]))(functools.partial(signal, peer))
    for load in loads:
        load.wait()
    pl.semaphore_wait(barrier, len(senders) + len(near) - edge.astype(jnp.int32))


class Layer:
    def __init__(self, step_count, row_count, width, group, head, context):
        self.step_count, self.row_count, self.width = step_count, row_count, width
        self.group, self.head, self.context = group, head, context
        self.tokens = step_count * row_count
        self.share = width // 8

    def scratch(self):
        rows, context, head = self.row_count, self.context, self.head
        features = self.group * head
        return [
            pltpu.VMEM((self.width, features), BF),
            pltpu.VMEM((self.width, head), BF),
            pltpu.VMEM((self.width, head), BF),
            pltpu.VMEM((features, self.width), BF),
            pltpu.VMEM((rows, context, head), BF),
            pltpu.VMEM((rows, context, head), BF),
            pltpu.VMEM((8, self.tokens, self.share), F32),
            pltpu.VMEM((8, self.tokens, self.share), F32),
            pltpu.VMEM((8, self.tokens, self.share), F32),
            pltpu.SemaphoreType.DMA((5 + 2 * rows,)),
            pltpu.SemaphoreType.DMA((14,)),
            pltpu.SemaphoreType.DMA((16,)),
        ]

    def begin(self, hidden, lengths, gain, sources, mixed, scratch):
        self.hidden, self.lengths, self.gain = hidden, lengths, gain
        self.w_query, self.w_key, self.w_value, self.w_out = scratch[:4]
        self.keys, self.values, self.partial, self.landed, self.mixed = scratch[4:9]
        loads, self.sent, self.got = scratch[9:]
        self.result = pltpu.make_async_copy(self.mixed, mixed, loads.at[4 + 2 * self.row_count])
        w_query, w_key, w_value, w_out, keys, values = sources
        pairs = [(w_query, self.w_query), (w_key, self.w_key), (w_value, self.w_value)]
        for r in range(self.row_count):
            pairs.append((keys.at[r, 0], self.keys.at[r]))
            pairs.append((values.at[r, 0], self.values.at[r]))
        pairs.append((w_out, self.w_out))
        self.loads = [pltpu.make_async_copy(a, b, loads.at[i]) for i, (a, b) in enumerate(pairs)]
        for load in self.loads:
            load.start()
        self.ends = []
        self.rows = {}

    def normalize(self):
        values = jnp.concatenate([self.hidden[s] for s in range(self.step_count)], axis=0).astype(F32)
        scale = lax.rsqrt(jnp.mean(values * values, axis=-1, keepdims=True) + 1e-06)
        self.normed = (values * scale * self.gain[...]).astype(BF)

    def turn(self):
        steps, rows, half = self.step_count, self.row_count, self.head // 2
        token = lax.broadcasted_iota(jnp.int32, (self.tokens, self.head), 0)
        lane = lax.broadcasted_iota(jnp.int32, (self.tokens, self.head), 1)
        position = token // rows
        for r in range(rows):
            position = position + jnp.where(token % rows == r, self.lengths[r], 0)
        power = (lane % half).astype(F32) * (2.0 / self.head)
        angles = position.astype(F32) * jnp.exp(-power * math.log(1000000.0))
        self.cosine = jnp.cos(angles)
        sine = jnp.sin(angles)
        self.sine = jnp.where(lane < half, -sine, sine)

    def rotate(self, vectors):
        return (vectors * self.cosine + pltpu.roll(vectors, self.head // 2, 1) * self.sine).astype(BF)

    def project_query(self, g):
        if g == 0:
            self.loads[0].wait()
            self.query = []
        at = g * self.head
        wide = jnp.dot(self.normed, self.w_query[:, at : at + self.head], preferred_element_type=F32)
        self.query.append(self.rotate(wide))

    def project_query_pair(self, g):
        if g == 0:
            self.loads[0].wait()
            self.query = []
        at = g * self.head
        wide = jnp.dot(self.normed, self.w_query[:, at : at + 2 * self.head], preferred_element_type=F32)
        self.query.append(self.rotate(wide[:, : self.head]))
        self.query.append(self.rotate(wide[:, self.head :]))

    def project_key(self):
        self.loads[1].wait()
        self.fresh_key = self.rotate(jnp.dot(self.normed, self.w_key[...], preferred_element_type=F32))

    def project_value(self):
        self.loads[2].wait()
        self.fresh_value = jnp.dot(self.normed, self.w_value[...], preferred_element_type=F32).astype(BF)

    def pick(self, size, total, test):
        out = lax.broadcasted_iota(jnp.int32, (size, total), 0)
        inner = lax.broadcasted_iota(jnp.int32, (size, total), 1)
        return test(out, inner).astype(F32).astype(BF)

    def score(self, r):
        self.loads[3 + 2 * r].wait()
        steps, rows, tokens = self.step_count, self.row_count, self.tokens
        heads = self.group * steps
        every = jnp.concatenate(self.query, axis=0)
        chosen = self.pick(
            heads, self.group * tokens, lambda o, i: i == (o // steps) * tokens + (o % steps) * rows + r
        )
        query = jnp.dot(chosen, every, preferred_element_type=F32).astype(BF)
        scale = 1.0 / math.sqrt(self.head)
        along = (((1,), (1,)), ((), ()))
        cached = lax.dot_general(query, self.keys[r], along, preferred_element_type=F32) * scale
        slot = lax.broadcasted_iota(jnp.int32, cached.shape, 1)
        cached = jnp.where(slot < self.lengths[r], cached, -jnp.inf)
        recent = lax.dot_general(query, self.fresh_key, along, preferred_element_type=F32) * scale
        out = lax.broadcasted_iota(jnp.int32, recent.shape, 0)
        token = lax.broadcasted_iota(jnp.int32, recent.shape, 1)
        recent = jnp.where((token % rows == r) & (token // rows <= out % steps), recent, -jnp.inf)
        top = jnp.maximum(
            jnp.max(cached, axis=-1, keepdims=True), jnp.max(recent, axis=-1, keepdims=True)
        )
        cached_exp = jnp.exp(cached - top)
        recent_exp = jnp.exp(recent - top)
        total = jnp.sum(cached_exp, axis=-1, keepdims=True) + jnp.sum(recent_exp, axis=-1, keepdims=True)
        self.rows[r] = (cached_exp / total).astype(BF), (recent_exp / total).astype(BF)

    def attend(self, r):
        self.loads[4 + 2 * r].wait()
        cached, recent = self.rows[r]
        result = jnp.dot(cached, self.values[r], preferred_element_type=F32)
        result = result + jnp.dot(recent, self.fresh_value, preferred_element_type=F32)
        self.rows[r] = result.astype(BF)

    def lay_out(self):
        steps, rows, tokens = self.step_count, self.row_count, self.tokens
        heads = self.group * steps
        every = jnp.concatenate([self.rows[r] for r in range(rows)], axis=0)
        parts = []
        for g in range(self.group):
            chosen = self.pick(
                tokens, rows * heads, lambda o, i: i == (o % rows) * heads + g * steps + o // rows
            )
            parts.append(jnp.dot(chosen, every, preferred_element_type=F32).astype(BF))
        self.attended = jnp.concatenate(parts, axis=1)

    def project_out(self, t):
        if t == 0:
            self.loads[-1].wait()
        columns = slice(t * self.share, (t + 1) * self.share)
        self.partial[t] = jnp.dot(self.attended, self.w_out[:, columns], preferred_element_type=F32)

    def group_peers(self):
        dp, tp = lax.axis_index("dp"), lax.axis_index("tp")
        return [(dp, (tp + step) % 8) for step in range(1, 8)]

    def copy(self, source, target, sent, got, to):
        return pltpu.make_async_remote_copy(
            src_ref=source,
            dst_ref=target,
            send_sem=self.sent.at[sent],
            recv_sem=self.got.at[got],
            device_id=to,
            device_id_type=MESH,
        )

    def scatter(self):
        me = lax.axis_index("tp")
        for step, peer in enumerate(self.group_peers(), 1):
            copy = self.copy(self.partial.at[peer[1]], self.landed.at[step], step - 1, step, peer)
            copy.start()
            self.ends.append(copy.wait_send)

    def gather(self):
        me = lax.axis_index("tp")
        total = self.partial[me]
        for step, peer in enumerate(self.group_peers(), 1):
            self.copy(self.landed.at[step], self.landed.at[step], 0, step, peer).wait_recv()
            total = total + self.landed[step]
        self.mixed[me] = total
        for step, peer in enumerate(self.group_peers(), 1):
            copy = self.copy(self.mixed.at[me], self.mixed.at[me], 6 + step, 8 + step, peer)
            copy.start()
            self.ends.append(copy.wait_send)

    def collect(self):
        me = lax.axis_index("tp")
        for step, peer in enumerate(self.group_peers(), 1):
            owner = (me + 8 - step) % 8
            self.copy(self.mixed.at[owner], self.mixed.at[owner], 0, 8 + step, peer).wait_recv()
        self.result.start()
        self.ends.append(self.result.wait)

    def steps(self):
        steps = {"normalize": self.normalize, "turn": self.turn}
        for g in range(0, self.group, 2):
            steps[f"query{g}"] = functools.partial(self.project_query_pair, g)
        steps["key"] = self.project_key
        steps["value"] = self.project_value
        for r in range(self.row_count):
            steps[f"score{r}"] = functools.partial(self.score, r)
            steps[f"attend{r}"] = functools.partial(self.attend, r)
        steps["lay_out"] = self.lay_out
        for t in range(8):
            steps[f"out{t}"] = functools.partial(self.project_out, t)
        steps["scatter"] = self.scatter
        steps["gather"] = self.gather
        steps["collect"] = self.collect
        return steps

    def finish(self):
        for end in self.ends:
            end()


def kernel(gather, layer, *refs):
    lengths, hidden, gain, q, k, v = refs[:6]
    sources, (held, mixed) = refs[6:12], refs[12:14]
    moved, ring, small, sent, got, own, hidden_here, gain_here, lengths_here = refs[14:23]
    gather.begin(held, moved, ring, sent, got)
    high, low = q.shape[0], k.shape[0]
    pairs = [
        (q, moved.at[0, pl.ds(0, high), :]),
        (k, small.at[0]),
        (v, small.at[1]),
        (hidden, hidden_here),
        (gain, gain_here),
        (lengths, lengths_here),
    ]
    loads = [pltpu.make_async_copy(a, b, own.at[i]) for i, (a, b) in enumerate(pairs)]
    for load in loads:
        load.start()
    layer.begin(hidden_here, lengths_here, gain_here, sources, mixed, refs[23:])
    senders, near, edge = gather.greetings()
    greet(senders + layer.group_peers(), near, edge, loads)
    moved[0, pl.ds(high, 2 * low), :] = jnp.concatenate([small[0], small[1]], axis=0)
    steps = [*gather.steps().values(), *layer.steps().values()]
    for number in ORDER:
        steps[number]()
    gather.finish()
    layer.finish()


def write_out(held, mixed, q, k, v, out, low_k, low_v, sems):
    high, low = q.shape[3], k.shape[2] // 4
    copies = [pltpu.make_async_copy(held.at[:, :, :, pl.ds(0, high), :], q, sems.at[0])]
    copies[0].start()
    for at, (staged, target) in enumerate(((low_k, k), (low_v, v))):
        for core in range(2):
            for slot in range(2):
                rows = slice(high + at * low, high + (at + 1) * low)
                staged[core, slot] = jnp.concatenate([held[core, slot, x, rows, :] for x in range(4)], axis=0)
        copies.append(pltpu.make_async_copy(staged, target, sems.at[1 + at]))
        copies[-1].start()
    steps, rows, _ = out.shape
    share = mixed.shape[2]
    for t in range(mixed.shape[0]):
        for s in range(steps):
            out[s, :, t * share : (t + 1) * share] = mixed[t, s * rows : (s + 1) * rows, :].astype(BF)
    for copy in copies:
        copy.wait()


def on_device(
    hidden,
    lengths,
    norm_gain,
    w_query,
    key_weight_matrix,
    value_weight_matrix,
    w_out,
    key_cache,
    cached_value_rows,
    next_query,
    upcoming_key_weight,
    upcoming_value_weight,
):
    step_count, row_count, width = hidden.shape
    head = key_cache.shape[3]
    group = w_query.shape[1] // head
    context = key_cache.shape[2]
    tokens = step_count * row_count
    high, low = next_query.shape[0], upcoming_key_weight.shape[0]
    rows = high + 2 * low
    gather = Gather(rows, width)
    layer = Layer(step_count, row_count, width, group, head, context)
    vmem = pl.BlockSpec(memory_space=pltpu.VMEM)
    hbm = pl.BlockSpec(memory_space=pltpu.HBM)
    held, mixed = pl.pallas_call(
        functools.partial(kernel, gather, layer),
        out_shape=(
            jax.ShapeDtypeStruct((2, 2, 4, rows, width), BF),
            jax.ShapeDtypeStruct((8, tokens, width // 8), F32),
        ),
        in_specs=[hbm] * 12,
        out_specs=(pl.BlockSpec(memory_space=pl.ANY),) * 2,
        scratch_shapes=[
            *gather.scratch()[:2],
            pltpu.VMEM((2, low, width), BF),
            *gather.scratch()[2:],
            pltpu.SemaphoreType.DMA((6,)),
            pltpu.VMEM((step_count, row_count, width), BF),
            pltpu.VMEM((1, width), F32),
            pltpu.SMEM((row_count,), jnp.int32),
            *layer.scratch(),
        ],
        compiler_params=pltpu.CompilerParams(
            collective_id=0, has_side_effects=True, vmem_limit_bytes=VMEM_LIMIT
        ),
        cost_estimate=pl.CostEstimate(flops=10**9, bytes_accessed=40 * 2**20, transcendentals=10**5),
    )(
        *(
            pltpu.with_memory_space_constraint(each, pltpu.HBM)
            for each in (
                lengths,
                hidden,
                norm_gain.reshape(1, width),
                next_query,
                upcoming_key_weight,
                upcoming_value_weight,
                w_query,
                key_weight_matrix,
                value_weight_matrix,
                w_out,
                key_cache,
                cached_value_rows,
            )
        ),
    )
    q, k, v, mixed = pl.pallas_call(
        write_out,
        out_shape=(
            jax.ShapeDtypeStruct((2, 2, 4, high, width), BF),
            jax.ShapeDtypeStruct((2, 2, 4 * low, width), BF),
            jax.ShapeDtypeStruct((2, 2, 4 * low, width), BF),
            jax.ShapeDtypeStruct((step_count, row_count, width), BF),
        ),
        in_specs=[vmem] * 2,
        out_specs=(hbm, hbm, hbm, vmem),
        scratch_shapes=[
            pltpu.VMEM((2, 2, 4 * low, width), BF),
            pltpu.VMEM((2, 2, 4 * low, width), BF),
            pltpu.SemaphoreType.DMA((3,)),
        ],
        compiler_params=pltpu.CompilerParams(vmem_limit_bytes=16 * 2**20),
    )(
        pltpu.with_memory_space_constraint(held, pltpu.VMEM),
        pltpu.with_memory_space_constraint(mixed, pltpu.VMEM),
    )
    return mixed, q.reshape(-1, width), k.reshape(-1, width), v.reshape(-1, width)


def solution(mesh):
    in_specs = (
        P(None, "dp", None),
        P("dp"),
        P(),
        P(None, "tp"),
        P(None, "tp"),
        P(None, "tp"),
        P("tp", None),
        P("dp", "tp", None, None),
        P("dp", "tp", None, None),
        P(("dp", "tp"), None),
        P(("dp", "tp"), None),
        P(("dp", "tp"), None),
    )
    out_specs = (P(None, "dp", None), P("tp", None), P("tp", None), P("tp", None))
    return jax.shard_map(
        on_device, mesh=mesh, in_specs=in_specs, out_specs=out_specs, check_vma=False
    )
```

```python
import functools
import math

import jax
import jax.numpy as jnp
from jax import lax
from jax.experimental import pallas as pl
from jax.experimental.pallas import tpu as pltpu
from jax.sharding import PartitionSpec as P

MESH = pl.DeviceIdType.MESH
BF = jnp.bfloat16
F32 = jnp.float32

CROSS = 768
TURN = 2304
CROSS_PARTS = 2
TURN_PARTS = 4
LATE_PARTS = 3
VMEM_LIMIT = 36 * 2**20
ORDER = (
    42, 0, 56, 9, 70, 43, 84, 85, 18, 57, 86, 1, 24, 2, 44, 87, 71, 45, 10, 30, 11, 3, 88, 89, 19, 90, 58, 4,
    59, 5, 36, 91, 12, 92, 93, 25, 94, 46, 72, 13, 47, 95, 73, 48, 14, 50, 20, 96, 97, 31, 98, 60, 61, 62,
    64, 26, 99, 100, 101, 102, 6, 37, 103, 49, 74, 75, 76, 51, 52, 78, 104, 32, 105, 106, 15, 21, 63, 65, 66,
    107, 38, 27, 77, 79, 80, 7, 33, 53, 16, 22, 108, 39, 67, 28, 54, 81, 34, 68, 109, 40, 82, 8, 17, 23, 29,
    35, 41, 55, 69, 83,
)


def place():
    dp, tp = lax.axis_index("dp"), lax.axis_index("tp")
    return tp % 4, (dp // 8) * 2 + tp // 4, (dp // 2) % 4, dp % 2


def device(x, y, z, core):
    return ((y // 2) * 8 + z * 2 + core, (y % 2) * 4 + x)


def cut(start, width, parts):
    tiles = width // 128
    edges = [128 * (tiles * i // parts) for i in range(parts + 1)]
    return [(start + edges[i], edges[i + 1] - edges[i]) for i in range(parts)]


class Gather:
    def __init__(self, rows, width):
        self.rows, self.width = rows, width
        bounds = [(0, CROSS, CROSS_PARTS), (CROSS, TURN, TURN_PARTS)]
        self.late_at = CROSS + TURN
        bounds.append((self.late_at, width - self.late_at, LATE_PARTS))
        self.parts = [(kind, at, size) for kind, bound in enumerate(bounds) for at, size in cut(*bound)]
        self.count = len(self.parts) * 19

    def scratch(self):
        return [
            pltpu.VMEM((2, self.rows, self.width), BF),
            pltpu.VMEM((4, 2, self.rows, CROSS), BF),
            pltpu.VMEM((2, 4, self.rows, self.width - self.late_at), BF),
            pltpu.SemaphoreType.DMA((self.count,)),
            pltpu.SemaphoreType.DMA((self.count,)),
        ]

    def begin(self, held, moved, ring, late, sent, got):
        self.held, self.moved, self.ring, self.late, self.sent, self.got = held, moved, ring, late, sent, got
        self.x, self.y, self.z, self.core = place()
        self.edge = (self.y == 0) | (self.y == 3)
        self.middle = jnp.logical_not(self.edge)
        self.ends = []

    def greet(self, loads):
        x, y, z, core = self.x, self.y, self.z, self.core
        barrier = pltpu.get_barrier_semaphore()

        def signal(peers):
            for peer in peers:
                pl.semaphore_signal(barrier, inc=1, device_id=peer, device_id_type=MESH)

        def row(at_y, first=0):
            return [device((x + i) % 4, at_y, z, core) for i in range(first, 4)]

        signal([device(x, y, (z + i) % 4, core) for i in range(1, 4)] + [device(x, y, z, 1 - core)])
        signal(row(y, 1) + row(y // 2 * 2 + 1 - y % 2))
        pl.when(self.edge)(lambda: signal([device(x, 3 - y, z, core)]))
        pl.when(self.middle)(lambda: signal(row(y % 2 * 2) + row(y % 2 * 2 + 1)))
        for load in loads:
            load.wait()
        pl.semaphore_wait(barrier, 15 + self.edge.astype(jnp.int32))

    def send(self, source, target, sent, got, to, when=None):
        copy = pltpu.make_async_remote_copy(
            src_ref=source,
            dst_ref=target,
            send_sem=self.sent.at[sent],
            recv_sem=self.got.at[got],
            device_id=to,
            device_id_type=MESH,
        )
        if when is None:
            copy.start()
            self.ends.append(copy.wait_send)
        else:
            pl.when(when)(copy.start)
            self.ends.append(lambda: pl.when(when)(copy.wait_send))

    def arrive(self, target, got):
        pltpu.make_async_remote_copy(
            src_ref=target,
            dst_ref=target,
            send_sem=self.sent.at[0],
            recv_sem=self.got.at[got],
            device_id=device(self.x, self.y, self.z, 1 - self.core),
            device_id_type=MESH,
        ).wait_recv()

    def z_start(self, view, sent, got):
        own = view(0)
        self.send(own, own, sent, got, device(self.x, self.y, (self.z + 1) % 4, self.core))
        self.send(own, own, sent + 1, got + 1, device(self.x, self.y, (self.z + 3) % 4, self.core))

    def z_pass(self, view, sent, got, upward):
        near, step = (3, 1) if upward else (1, 3)
        piece = view(near)
        self.arrive(piece, got + (0 if upward else 1))
        self.send(piece, piece, sent + 2, got + 2, device(self.x, self.y, (self.z + step) % 4, self.core))

    def z_other(self, view, got, upward):
        self.arrive(view(1 if upward else 3), got + (1 if upward else 0))

    def z_far(self, view, got):
        self.arrive(view(2), got + 2)

    def both(self, view, target, sent, got, x, stays):
        y = self.y
        for which in range(2):
            goal_y = y // 2 + 2 * which
            here = stays & (goal_y == y)
            self.send(view, target, sent + which, got + y % 2, device(x, goal_y, self.z, self.core), jnp.logical_not(here))
            pl.when(here)(pltpu.make_async_copy(view, target, self.sent.at[sent + which]).start)

    def land(self, view, target, slot, sent, got, stays):
        y = self.y
        here = stays & (y % 2 * 2 + slot == y)
        pl.when(here)(pltpu.make_async_copy(view, target, self.sent.at[sent + y // 2]).wait)
        pl.when(jnp.logical_not(here))(lambda: self.arrive(target, got + slot))

    def share(self, whole, sem):
        self.send(whole(self.core), whole(self.core), sem, sem, device(self.x, self.y, self.z, 1 - self.core))

    def cross_steps(self, n):
        at, size = self.parts[n][1:]
        base = n * 19
        upward = n % 2 == 0
        x, y, z, core = self.x, self.y, self.z, self.core
        columns, slots = pl.ds(at, size), pl.ds(0, 2)
        here = jnp.bool_(True)
        first = self.moved.at[0, :, columns]
        view = lambda step: self.ring.at[(z + step) % 4, :, :, columns]
        at_z = lambda to_x: self.ring.at[to_x, :, :, columns]
        final = lambda from_x: self.held.at[core, slots, from_x, :, columns]
        whole = lambda core: self.held.at[core, slots, :, :, columns]

        def start():
            self.both(first, self.ring.at[z, y % 2, :, columns], base, base, x, here)

        def column():
            for slot in range(2):
                self.land(first, self.ring.at[z, slot, :, columns], slot, base, base, here)
            self.z_start(view, base + 2, base + 2)

        def cross(step):
            goal = (z + step) % 4
            hops = (goal - x + 4) % 4
            to = device(goal, y, z, core)
            self.send(at_z(goal), final(x), base + 5 + step, base + 4 + hops, to, hops != 0)
            stay = pltpu.make_async_copy(at_z(goal), final(x), self.sent.at[base + 5 + step])
            pl.when(hops == 0)(stay.start)

        def relay():
            self.z_pass(view, base + 2, base + 2, upward)

        def second():
            self.z_other(view, base + 2, upward)
            cross(1 if upward else 3)

        def far():
            self.z_far(view, base + 2)
            cross(2)

        def finish():
            step = (x - z + 4) % 4
            pltpu.make_async_copy(at_z(x), final(x), self.sent.at[base + 5 + step]).wait()
            for hops in range(1, 4):
                self.arrive(final((x + 4 - hops) % 4), base + 4 + hops)
            self.share(whole, base + 9)

        def done():
            self.arrive(whole(1 - core), base + 9)

        return [
            ("start", start),
            ("column", column),
            ("cross0", functools.partial(cross, 0)),
            ("relay", relay),
            ("cross1", functools.partial(cross, 3 if upward else 1)),
            ("second", second),
            ("far", far),
            ("finish", finish),
            ("done", done),
        ]

    def turn_steps(self, n):
        at, size = self.parts[n][1:]
        base = n * 19
        upward = n % 2 == 0
        x, y, z, core = self.x, self.y, self.z, self.core
        columns, slots = pl.ds(at, size), pl.ds(0, 2)
        shift = (x + n) % 4
        goal = (z + 8 - x - n % 4) % 4
        at_x = lambda step: (z + step + 8 - x - n % 4) % 4
        pair = lambda step: self.held.at[core, slots, at_x(step), :, columns]
        whole = lambda core: self.held.at[core, slots, :, :, columns]
        first, shifted = (self.moved.at[slot, :, columns] for slot in range(2))
        view = self.moved.at[jnp.where(shift == 0, 0, 1), :, columns]

        def start():
            self.send(first, shifted, base, base, device(x, y, (z + shift) % 4, core), shift != 0)

        def turn():
            pl.when(shift != 0)(lambda: self.arrive(shifted, base))
            self.both(view, self.held.at[core, y % 2, x, :, columns], base + 1, base + 1, goal, goal == x)

        def column():
            for slot in range(2):
                target = self.held.at[core, slot, at_x(0), :, columns]
                self.land(view, target, slot, base + 1, base + 1, at_x(0) == x)
            self.z_start(pair, base + 3, base + 3)

        def relay():
            self.z_pass(pair, base + 3, base + 3, upward)

        def finish():
            self.z_other(pair, base + 3, upward)
            self.z_far(pair, base + 3)
            self.share(whole, base + 9)

        def done():
            self.arrive(whole(1 - core), base + 9)

        return [
            ("start", start),
            ("turn", turn),
            ("column", column),
            ("relay", relay),
            ("finish", finish),
            ("done", done),
        ]

    def late_steps(self, n):
        at, size = self.parts[n][1:]
        base = n * 19
        upward = n % 2 == 0
        x, y, z, core = self.x, self.y, self.z, self.core
        columns, local, slots = pl.ds(at, size), pl.ds(at - self.late_at, size), pl.ds(0, 2)
        shift = (x + n) % 4
        goal = (z + 8 - x - n % 4) % 4
        at_x = lambda step: (z + step + 8 - x - n % 4) % 4
        own = lambda step: self.late.at[0, at_x(step), :, local]
        passing = lambda step: self.late.at[1, at_x(step), :, local]
        piece = lambda slot, step: self.held.at[core, slot, at_x(step), :, columns]
        whole = lambda core: self.held.at[core, slots, :, :, columns]
        first, shifted = (self.moved.at[slot, :, columns] for slot in range(2))
        view = self.moved.at[jnp.where(shift == 0, 0, 1), :, columns]
        inner = jnp.where((y == 0) | (y == 2), 1, 2)
        slot = jnp.where((y == 0) | (y == 1), 1, 0)
        keep = pltpu.make_async_copy(
            self.late.at[0, :, :, local], self.held.at[core, y // 3, :, :, columns], self.sent.at[base + 17]
        )

        def start():
            self.send(first, shifted, base, base, device(x, y, (z + shift) % 4, core), shift != 0)

        def turn():
            pl.when(shift != 0)(lambda: self.arrive(shifted, base))
            target = self.late.at[0, x, :, local]
            self.send(view, target, base + 1, base + 1, device(goal, y, z, core), goal != x)
            pl.when(goal == x)(pltpu.make_async_copy(view, target, self.sent.at[base + 1]).start)

        def column():
            pl.when(goal == x)(pltpu.make_async_copy(view, own(0), self.sent.at[base + 1]).wait)
            pl.when(goal != x)(lambda: self.arrive(own(0), base + 1))
            self.z_start(own, base + 2, base + 2)

        def spread(step):
            sem = base + 5 + step
            self.send(own(step), passing(step), sem, base + 13 + step, device(x, 3 - y, z, core), self.edge)
            got = base + 5 + 4 * slot + step
            outer = device(x, y // 2 * 3, z, core)
            self.send(own(step), piece(slot, step), sem, got, outer, self.middle)
            self.send(own(step), piece(slot, step), sem + 4, got, device(x, inner, z, core), self.middle)

        def passed(step):
            pl.when(self.edge)(lambda: self.arrive(passing(step), base + 13 + step))
            got = base + 5 + 4 * slot + step
            self.send(passing(step), piece(slot, step), base + 9 + step, got, device(x, inner, z, core), self.edge)

        def relay():
            self.z_pass(own, base + 2, base + 2, upward)

        def second():
            self.z_other(own, base + 2, upward)
            spread(1 if upward else 3)

        def far():
            self.z_far(own, base + 2)
            spread(2)
            pl.when(self.edge)(keep.start)

        def finish():
            def arrived(slot):
                for step in range(4):
                    self.arrive(piece(slot, step), base + 5 + 4 * slot + step)

            def at_edge():
                arrived(1 - y // 3)
                keep.wait()

            def at_middle():
                arrived(0)
                arrived(1)

            pl.when(self.edge)(at_edge)
            pl.when(self.middle)(at_middle)
            self.share(whole, base + 18)

        def done():
            self.arrive(whole(1 - core), base + 18)

        near = 3 if upward else 1
        return [
            ("start", start),
            ("turn", turn),
            ("column", column),
            ("spread0", functools.partial(spread, 0)),
            ("relay", relay),
            ("spread1", functools.partial(spread, near)),
            ("second", second),
            ("far", far),
            ("passed0", functools.partial(passed, 0)),
            ("passed1", functools.partial(passed, near)),
            ("passed2", functools.partial(passed, 4 - near)),
            ("passed3", functools.partial(passed, 2)),
            ("finish", finish),
            ("done", done),
        ]

    def steps(self):
        steps = {}
        for n, part in enumerate(self.parts):
            made = (self.cross_steps, self.turn_steps, self.late_steps)[part[0]](n)
            steps.update({f"{n}.{name}": step for name, step in made})
        return steps

    def finish(self):
        for end in self.ends:
            end()


class Layer:
    def __init__(self, step_count, row_count, width, group, head, context):
        self.step_count, self.row_count, self.width = step_count, row_count, width
        self.group, self.head, self.context = group, head, context
        self.tokens = step_count * row_count
        self.share = width // 8

    def scratch(self):
        rows, context, head = self.row_count, self.context, self.head
        features = self.group * head
        return [
            pltpu.VMEM((self.width, features), BF),
            pltpu.VMEM((self.width, head), BF),
            pltpu.VMEM((self.width, head), BF),
            pltpu.VMEM((features, self.width), BF),
            pltpu.VMEM((rows, context, head), BF),
            pltpu.VMEM((rows, context, head), BF),
            pltpu.VMEM((8, self.tokens, self.share), F32),
            pltpu.VMEM((8, self.tokens, self.share), F32),
            pltpu.VMEM((8, self.tokens, self.share), F32),
            pltpu.SemaphoreType.DMA((5 + 2 * rows,)),
            pltpu.SemaphoreType.DMA((14,)),
            pltpu.SemaphoreType.DMA((16,)),
        ]

    def begin(self, hidden, lengths, gain, sources, mixed, scratch):
        self.hidden, self.lengths, self.gain = hidden, lengths, gain
        self.w_query, self.w_key, self.w_value, self.w_out = scratch[:4]
        self.keys, self.values, self.partial, self.landed, self.mixed = scratch[4:9]
        loads, self.sent, self.got = scratch[9:]
        self.result = pltpu.make_async_copy(self.mixed, mixed, loads.at[4 + 2 * self.row_count])
        w_query, w_key, w_value, w_out, keys, values = sources
        pairs = [(w_query, self.w_query), (w_key, self.w_key), (w_value, self.w_value)]
        for r in range(self.row_count):
            pairs.append((keys.at[r, 0], self.keys.at[r]))
            pairs.append((values.at[r, 0], self.values.at[r]))
        pairs.append((w_out, self.w_out))
        self.loads = [pltpu.make_async_copy(a, b, loads.at[i]) for i, (a, b) in enumerate(pairs)]
        for load in self.loads:
            load.start()
        self.ends = []
        self.rows = {}

    def normalize(self):
        values = jnp.concatenate([self.hidden[s] for s in range(self.step_count)], axis=0).astype(F32)
        scale = lax.rsqrt(jnp.mean(values * values, axis=-1, keepdims=True) + 1e-06)
        self.normed = (values * scale * self.gain[...]).astype(BF)

    def turn(self):
        steps, rows, half = self.step_count, self.row_count, self.head // 2
        token = lax.broadcasted_iota(jnp.int32, (self.tokens, self.head), 0)
        lane = lax.broadcasted_iota(jnp.int32, (self.tokens, self.head), 1)
        position = token // rows
        for r in range(rows):
            position = position + jnp.where(token % rows == r, self.lengths[r], 0)
        power = (lane % half).astype(F32) * (2.0 / self.head)
        angles = position.astype(F32) * jnp.exp(-power * math.log(1000000.0))
        self.cosine = jnp.cos(angles)
        sine = jnp.sin(angles)
        self.sine = jnp.where(lane < half, -sine, sine)

    def rotate(self, vectors):
        return (vectors * self.cosine + pltpu.roll(vectors, self.head // 2, 1) * self.sine).astype(BF)

    def project_query(self, g):
        if g == 0:
            self.loads[0].wait()
            self.query = []
        at = g * self.head
        wide = jnp.dot(self.normed, self.w_query[:, at : at + self.head], preferred_element_type=F32)
        self.query.append(self.rotate(wide))

    def project_query_pair(self, g):
        if g == 0:
            self.loads[0].wait()
            self.query = []
        at = g * self.head
        wide = jnp.dot(self.normed, self.w_query[:, at : at + 2 * self.head], preferred_element_type=F32)
        self.query.append(self.rotate(wide[:, : self.head]))
        self.query.append(self.rotate(wide[:, self.head :]))

    def project_key(self):
        self.loads[1].wait()
        self.fresh_key = self.rotate(jnp.dot(self.normed, self.w_key[...], preferred_element_type=F32))

    def project_value(self):
        self.loads[2].wait()
        self.fresh_value = jnp.dot(self.normed, self.w_value[...], preferred_element_type=F32).astype(BF)

    def pick(self, size, total, test):
        out = lax.broadcasted_iota(jnp.int32, (size, total), 0)
        inner = lax.broadcasted_iota(jnp.int32, (size, total), 1)
        return test(out, inner).astype(F32).astype(BF)

    def score(self, r):
        self.loads[3 + 2 * r].wait()
        steps, rows, tokens = self.step_count, self.row_count, self.tokens
        heads = self.group * steps
        every = jnp.concatenate(self.query, axis=0)
        chosen = self.pick(
            heads, self.group * tokens, lambda o, i: i == (o // steps) * tokens + (o % steps) * rows + r
        )
        query = jnp.dot(chosen, every, preferred_element_type=F32).astype(BF)
        scale = 1.0 / math.sqrt(self.head)
        along = (((1,), (1,)), ((), ()))
        cached = lax.dot_general(query, self.keys[r], along, preferred_element_type=F32) * scale
        slot = lax.broadcasted_iota(jnp.int32, cached.shape, 1)
        cached = jnp.where(slot < self.lengths[r], cached, -jnp.inf)
        recent = lax.dot_general(query, self.fresh_key, along, preferred_element_type=F32) * scale
        out = lax.broadcasted_iota(jnp.int32, recent.shape, 0)
        token = lax.broadcasted_iota(jnp.int32, recent.shape, 1)
        recent = jnp.where((token % rows == r) & (token // rows <= out % steps), recent, -jnp.inf)
        top = jnp.maximum(
            jnp.max(cached, axis=-1, keepdims=True), jnp.max(recent, axis=-1, keepdims=True)
        )
        cached_exp = jnp.exp(cached - top)
        recent_exp = jnp.exp(recent - top)
        total = jnp.sum(cached_exp, axis=-1, keepdims=True) + jnp.sum(recent_exp, axis=-1, keepdims=True)
        self.rows[r] = (cached_exp / total).astype(BF), (recent_exp / total).astype(BF)

    def attend(self, r):
        self.loads[4 + 2 * r].wait()
        cached, recent = self.rows[r]
        result = jnp.dot(cached, self.values[r], preferred_element_type=F32)
        result = result + jnp.dot(recent, self.fresh_value, preferred_element_type=F32)
        self.rows[r] = result.astype(BF)

    def lay_out(self):
        steps, rows, tokens = self.step_count, self.row_count, self.tokens
        heads = self.group * steps
        every = jnp.concatenate([self.rows[r] for r in range(rows)], axis=0)
        parts = []
        for g in range(self.group):
            chosen = self.pick(
                tokens, rows * heads, lambda o, i: i == (o % rows) * heads + g * steps + o // rows
            )
            parts.append(jnp.dot(chosen, every, preferred_element_type=F32).astype(BF))
        self.attended = jnp.concatenate(parts, axis=1)

    def project_out(self, t):
        if t == 0:
            self.loads[-1].wait()
        columns = slice(t * self.share, (t + 1) * self.share)
        self.partial[t] = jnp.dot(self.attended, self.w_out[:, columns], preferred_element_type=F32)

    def group_peers(self):
        dp, tp = lax.axis_index("dp"), lax.axis_index("tp")
        return [(dp, (tp + step) % 8) for step in range(1, 8)]

    def copy(self, source, target, sent, got, to):
        return pltpu.make_async_remote_copy(
            src_ref=source,
            dst_ref=target,
            send_sem=self.sent.at[sent],
            recv_sem=self.got.at[got],
            device_id=to,
            device_id_type=MESH,
        )

    def scatter(self):
        me = lax.axis_index("tp")
        for step, peer in enumerate(self.group_peers(), 1):
            copy = self.copy(self.partial.at[peer[1]], self.landed.at[step], step - 1, step, peer)
            copy.start()
            self.ends.append(copy.wait_send)

    def gather(self):
        me = lax.axis_index("tp")
        total = self.partial[me]
        for step, peer in enumerate(self.group_peers(), 1):
            self.copy(self.landed.at[step], self.landed.at[step], 0, step, peer).wait_recv()
            total = total + self.landed[step]
        self.mixed[me] = total
        for step, peer in enumerate(self.group_peers(), 1):
            copy = self.copy(self.mixed.at[me], self.mixed.at[me], 6 + step, 8 + step, peer)
            copy.start()
            self.ends.append(copy.wait_send)

    def collect(self):
        me = lax.axis_index("tp")
        for step, peer in enumerate(self.group_peers(), 1):
            owner = (me + 8 - step) % 8
            self.copy(self.mixed.at[owner], self.mixed.at[owner], 0, 8 + step, peer).wait_recv()
        self.result.start()
        self.ends.append(self.result.wait)

    def steps(self):
        steps = {"normalize": self.normalize, "turn": self.turn}
        for g in range(0, self.group, 2):
            steps[f"query{g}"] = functools.partial(self.project_query_pair, g)
        steps["key"] = self.project_key
        steps["value"] = self.project_value
        for r in range(self.row_count):
            steps[f"score{r}"] = functools.partial(self.score, r)
            steps[f"attend{r}"] = functools.partial(self.attend, r)
        steps["lay_out"] = self.lay_out
        for t in range(8):
            steps[f"out{t}"] = functools.partial(self.project_out, t)
        steps["scatter"] = self.scatter
        steps["gather"] = self.gather
        steps["collect"] = self.collect
        return steps

    def finish(self):
        for end in self.ends:
            end()


def kernel(gather, layer, *refs):
    lengths, hidden, gain, q, k, v = refs[:6]
    sources, (held, mixed) = refs[6:12], refs[12:14]
    moved, ring, late, small, sent, got, own, hidden_here, gain_here, lengths_here = refs[14:24]
    gather.begin(held, moved, ring, late, sent, got)
    high, low = q.shape[0], k.shape[0]
    pairs = [
        (q, moved.at[0, pl.ds(0, high), :]),
        (k, small.at[0]),
        (v, small.at[1]),
        (hidden, hidden_here),
        (gain, gain_here),
        (lengths, lengths_here),
    ]
    loads = [pltpu.make_async_copy(a, b, own.at[i]) for i, (a, b) in enumerate(pairs)]
    for load in loads:
        load.start()
    layer.begin(hidden_here, lengths_here, gain_here, sources, mixed, refs[24:])
    gather.greet(loads)
    moved[0, pl.ds(high, 2 * low), :] = jnp.concatenate([small[0], small[1]], axis=0)
    steps = [*gather.steps().values(), *layer.steps().values()]
    for number in ORDER:
        steps[number]()
    gather.finish()
    layer.finish()


def write_out(held, mixed, q, k, v, out, low_k, low_v, sems):
    high, low = q.shape[3], k.shape[2] // 4
    copies = [pltpu.make_async_copy(held.at[:, :, :, pl.ds(0, high), :], q, sems.at[0])]
    copies[0].start()
    for core in range(2):
        for slot in range(2):
            for at, (staged, target) in enumerate(((low_k, k), (low_v, v))):
                rows = slice(high + at * low, high + (at + 1) * low)
                staged[core, slot] = jnp.concatenate([held[core, slot, x, rows, :] for x in range(4)], axis=0)
                part = (core, slot)
                copies.append(pltpu.make_async_copy(staged.at[part], target.at[part], sems.at[len(copies)]))
                copies[-1].start()
    steps, rows, _ = out.shape
    share = mixed.shape[2]
    for t in range(mixed.shape[0]):
        for s in range(steps):
            out[s, :, t * share : (t + 1) * share] = mixed[t, s * rows : (s + 1) * rows, :].astype(BF)
    for copy in copies:
        copy.wait()


def on_device(
    hidden,
    lengths,
    norm_gain,
    w_query,
    key_weight_matrix,
    value_weight_matrix,
    w_out,
    key_cache,
    cached_value_rows,
    next_query,
    upcoming_key_weight,
    upcoming_value_weight,
):
    step_count, row_count, width = hidden.shape
    head = key_cache.shape[3]
    group = w_query.shape[1] // head
    context = key_cache.shape[2]
    tokens = step_count * row_count
    high, low = next_query.shape[0], upcoming_key_weight.shape[0]
    rows = high + 2 * low
    gather = Gather(rows, width)
    layer = Layer(step_count, row_count, width, group, head, context)
    vmem = pl.BlockSpec(memory_space=pltpu.VMEM)
    hbm = pl.BlockSpec(memory_space=pltpu.HBM)
    held, mixed = pl.pallas_call(
        functools.partial(kernel, gather, layer),
        out_shape=(
            jax.ShapeDtypeStruct((2, 2, 4, rows, width), BF),
            jax.ShapeDtypeStruct((8, tokens, width // 8), F32),
        ),
        in_specs=[hbm] * 12,
        out_specs=(pl.BlockSpec(memory_space=pl.ANY),) * 2,
        scratch_shapes=[
            *gather.scratch()[:3],
            pltpu.VMEM((2, low, width), BF),
            *gather.scratch()[3:],
            pltpu.SemaphoreType.DMA((6,)),
            pltpu.VMEM((step_count, row_count, width), BF),
            pltpu.VMEM((1, width), F32),
            pltpu.SMEM((row_count,), jnp.int32),
            *layer.scratch(),
        ],
        compiler_params=pltpu.CompilerParams(
            collective_id=0, has_side_effects=True, vmem_limit_bytes=VMEM_LIMIT
        ),
        cost_estimate=pl.CostEstimate(flops=10**9, bytes_accessed=40 * 2**20, transcendentals=10**5),
    )(
        *(
            pltpu.with_memory_space_constraint(each, pltpu.HBM)
            for each in (
                lengths,
                hidden,
                norm_gain.reshape(1, width),
                next_query,
                upcoming_key_weight,
                upcoming_value_weight,
                w_query,
                key_weight_matrix,
                value_weight_matrix,
                w_out,
                key_cache,
                cached_value_rows,
            )
        ),
    )
    q, k, v, mixed = pl.pallas_call(
        write_out,
        out_shape=(
            jax.ShapeDtypeStruct((2, 2, 4, high, width), BF),
            jax.ShapeDtypeStruct((2, 2, 4 * low, width), BF),
            jax.ShapeDtypeStruct((2, 2, 4 * low, width), BF),
            jax.ShapeDtypeStruct((step_count, row_count, width), BF),
        ),
        in_specs=[vmem] * 2,
        out_specs=(hbm, hbm, hbm, vmem),
        scratch_shapes=[
            pltpu.VMEM((2, 2, 4 * low, width), BF),
            pltpu.VMEM((2, 2, 4 * low, width), BF),
            pltpu.SemaphoreType.DMA((9,)),
        ],
        compiler_params=pltpu.CompilerParams(vmem_limit_bytes=16 * 2**20),
    )(
        pltpu.with_memory_space_constraint(held, pltpu.VMEM),
        pltpu.with_memory_space_constraint(mixed, pltpu.VMEM),
    )
    return mixed, q.reshape(-1, width), k.reshape(-1, width), v.reshape(-1, width)


def solution(mesh):
    in_specs = (
        P(None, "dp", None),
        P("dp"),
        P(),
        P(None, "tp"),
        P(None, "tp"),
        P(None, "tp"),
        P("tp", None),
        P("dp", "tp", None, None),
        P("dp", "tp", None, None),
        P(("dp", "tp"), None),
        P(("dp", "tp"), None),
        P(("dp", "tp"), None),
    )
    out_specs = (P(None, "dp", None), P("tp", None), P("tp", None), P("tp", None))
    return jax.shard_map(
        on_device, mesh=mesh, in_specs=in_specs, out_specs=out_specs, check_vma=False
    )
```

```python
import functools
import math

import jax
import jax.numpy as jnp
from jax import lax
from jax.experimental import pallas as pl
from jax.experimental.pallas import tpu as pltpu
from jax.sharding import PartitionSpec as P

MESH = pl.DeviceIdType.MESH
BF = jnp.bfloat16
F32 = jnp.float32

CROSS = 640
TURN = 2432
CROSS_PARTS = 2
TURN_PARTS = 4
LATE_PARTS = 3
VMEM_LIMIT = 36 * 2**20
ORDER = (
    42, 0, 56, 9, 70, 18, 43, 84, 85, 24, 57, 86, 1, 30, 2, 44, 87, 45, 71, 10, 19, 36, 11, 58, 88, 89, 59,
    3, 4, 5, 25, 90, 46, 72, 91, 47, 73, 48, 50, 92, 12, 93, 20, 13, 94, 95, 14, 31, 60, 96, 61, 62, 64, 26,
    97, 98, 99, 37, 49, 100, 74, 75, 76, 51, 52, 78, 101, 6, 32, 102, 103, 104, 21, 63, 65, 66, 105, 15, 38,
    106, 107, 27, 77, 79, 80, 53, 7, 33, 67, 16, 22, 108, 39, 54, 81, 28, 68, 34, 82, 40, 109, 8, 17, 23, 29,
    35, 41, 55, 69, 83,
)


def place():
    dp, tp = lax.axis_index("dp"), lax.axis_index("tp")
    return tp % 4, (dp // 8) * 2 + tp // 4, (dp // 2) % 4, dp % 2


def device(x, y, z, core):
    return ((y // 2) * 8 + z * 2 + core, (y % 2) * 4 + x)


def cut(start, width, parts):
    tiles = width // 128
    edges = [128 * (tiles * i // parts) for i in range(parts + 1)]
    return [(start + edges[i], edges[i + 1] - edges[i]) for i in range(parts)]


class Gather:
    def __init__(self, rows, width):
        self.rows, self.width = rows, width
        bounds = [(0, CROSS, CROSS_PARTS), (CROSS, TURN, TURN_PARTS)]
        self.late_at = CROSS + TURN
        bounds.append((self.late_at, width - self.late_at, LATE_PARTS))
        self.parts = [(kind, at, size) for kind, bound in enumerate(bounds) for at, size in cut(*bound)]
        self.count = len(self.parts) * 19

    def scratch(self):
        return [
            pltpu.VMEM((2, self.rows, self.width), BF),
            pltpu.VMEM((4, 2, self.rows, CROSS), BF),
            pltpu.VMEM((2, 4, self.rows, self.width - self.late_at), BF),
            pltpu.SemaphoreType.DMA((self.count,)),
            pltpu.SemaphoreType.DMA((self.count,)),
        ]

    def begin(self, held, moved, ring, late, sent, got):
        self.held, self.moved, self.ring, self.late, self.sent, self.got = held, moved, ring, late, sent, got
        self.x, self.y, self.z, self.core = place()
        self.edge = (self.y == 0) | (self.y == 3)
        self.middle = jnp.logical_not(self.edge)
        self.ends = []

    def greet(self, loads):
        x, y, z, core = self.x, self.y, self.z, self.core
        barrier = pltpu.get_barrier_semaphore()

        def signal(peers):
            for peer in peers:
                pl.semaphore_signal(barrier, inc=1, device_id=peer, device_id_type=MESH)

        def row(at_y, first=0):
            return [device((x + i) % 4, at_y, z, core) for i in range(first, 4)]

        signal([device(x, y, (z + i) % 4, core) for i in range(1, 4)] + [device(x, y, z, 1 - core)])
        signal(row(y, 1) + row(y // 2 * 2 + 1 - y % 2))
        pl.when(self.edge)(lambda: signal([device(x, 3 - y, z, core)]))
        pl.when(self.middle)(lambda: signal(row(y % 2 * 2) + row(y % 2 * 2 + 1)))
        for load in loads:
            load.wait()
        pl.semaphore_wait(barrier, 15 + self.edge.astype(jnp.int32))

    def send(self, source, target, sent, got, to, when=None):
        copy = pltpu.make_async_remote_copy(
            src_ref=source,
            dst_ref=target,
            send_sem=self.sent.at[sent],
            recv_sem=self.got.at[got],
            device_id=to,
            device_id_type=MESH,
        )
        if when is None:
            copy.start()
            self.ends.append(copy.wait_send)
        else:
            pl.when(when)(copy.start)
            self.ends.append(lambda: pl.when(when)(copy.wait_send))

    def arrive(self, target, got):
        pltpu.make_async_remote_copy(
            src_ref=target,
            dst_ref=target,
            send_sem=self.sent.at[0],
            recv_sem=self.got.at[got],
            device_id=device(self.x, self.y, self.z, 1 - self.core),
            device_id_type=MESH,
        ).wait_recv()

    def z_start(self, view, sent, got):
        own = view(0)
        self.send(own, own, sent, got, device(self.x, self.y, (self.z + 1) % 4, self.core))
        self.send(own, own, sent + 1, got + 1, device(self.x, self.y, (self.z + 3) % 4, self.core))

    def z_pass(self, view, sent, got, upward):
        near, step = (3, 1) if upward else (1, 3)
        piece = view(near)
        self.arrive(piece, got + (0 if upward else 1))
        self.send(piece, piece, sent + 2, got + 2, device(self.x, self.y, (self.z + step) % 4, self.core))

    def z_other(self, view, got, upward):
        self.arrive(view(1 if upward else 3), got + (1 if upward else 0))

    def z_far(self, view, got):
        self.arrive(view(2), got + 2)

    def both(self, view, target, sent, got, x, stays):
        y = self.y
        for which in range(2):
            goal_y = y // 2 + 2 * which
            here = stays & (goal_y == y)
            self.send(view, target, sent + which, got + y % 2, device(x, goal_y, self.z, self.core), jnp.logical_not(here))
            pl.when(here)(pltpu.make_async_copy(view, target, self.sent.at[sent + which]).start)

    def land(self, view, target, slot, sent, got, stays):
        y = self.y
        here = stays & (y % 2 * 2 + slot == y)
        pl.when(here)(pltpu.make_async_copy(view, target, self.sent.at[sent + y // 2]).wait)
        pl.when(jnp.logical_not(here))(lambda: self.arrive(target, got + slot))

    def share(self, whole, sem):
        self.send(whole(self.core), whole(self.core), sem, sem, device(self.x, self.y, self.z, 1 - self.core))

    def cross_steps(self, n):
        at, size = self.parts[n][1:]
        base = n * 19
        upward = n % 2 == 0
        x, y, z, core = self.x, self.y, self.z, self.core
        columns, slots = pl.ds(at, size), pl.ds(0, 2)
        here = jnp.bool_(True)
        first = self.moved.at[0, :, columns]
        view = lambda step: self.ring.at[(z + step) % 4, :, :, columns]
        at_z = lambda to_x: self.ring.at[to_x, :, :, columns]
        final = lambda from_x: self.held.at[core, slots, from_x, :, columns]
        whole = lambda core: self.held.at[core, slots, :, :, columns]

        def start():
            self.both(first, self.ring.at[z, y % 2, :, columns], base, base, x, here)

        def column():
            for slot in range(2):
                self.land(first, self.ring.at[z, slot, :, columns], slot, base, base, here)
            self.z_start(view, base + 2, base + 2)

        def cross(step):
            goal = (z + step) % 4
            hops = (goal - x + 4) % 4
            to = device(goal, y, z, core)
            self.send(at_z(goal), final(x), base + 5 + step, base + 4 + hops, to, hops != 0)
            stay = pltpu.make_async_copy(at_z(goal), final(x), self.sent.at[base + 5 + step])
            pl.when(hops == 0)(stay.start)

        def relay():
            self.z_pass(view, base + 2, base + 2, upward)

        def second():
            self.z_other(view, base + 2, upward)
            cross(1 if upward else 3)

        def far():
            self.z_far(view, base + 2)
            cross(2)

        def finish():
            step = (x - z + 4) % 4
            pltpu.make_async_copy(at_z(x), final(x), self.sent.at[base + 5 + step]).wait()
            for hops in range(1, 4):
                self.arrive(final((x + 4 - hops) % 4), base + 4 + hops)
            self.share(whole, base + 9)

        def done():
            self.arrive(whole(1 - core), base + 9)

        return [
            ("start", start),
            ("column", column),
            ("cross0", functools.partial(cross, 0)),
            ("relay", relay),
            ("cross1", functools.partial(cross, 3 if upward else 1)),
            ("second", second),
            ("far", far),
            ("finish", finish),
            ("done", done),
        ]

    def turn_steps(self, n):
        at, size = self.parts[n][1:]
        base = n * 19
        upward = n % 2 == 0
        x, y, z, core = self.x, self.y, self.z, self.core
        columns, slots = pl.ds(at, size), pl.ds(0, 2)
        shift = (x + n) % 4
        goal = (z + 8 - x - n % 4) % 4
        at_x = lambda step: (z + step + 8 - x - n % 4) % 4
        pair = lambda step: self.held.at[core, slots, at_x(step), :, columns]
        whole = lambda core: self.held.at[core, slots, :, :, columns]
        first, shifted = (self.moved.at[slot, :, columns] for slot in range(2))
        view = self.moved.at[jnp.where(shift == 0, 0, 1), :, columns]

        def start():
            self.send(first, shifted, base, base, device(x, y, (z + shift) % 4, core), shift != 0)

        def turn():
            pl.when(shift != 0)(lambda: self.arrive(shifted, base))
            self.both(view, self.held.at[core, y % 2, x, :, columns], base + 1, base + 1, goal, goal == x)

        def column():
            for slot in range(2):
                target = self.held.at[core, slot, at_x(0), :, columns]
                self.land(view, target, slot, base + 1, base + 1, at_x(0) == x)
            self.z_start(pair, base + 3, base + 3)

        def relay():
            self.z_pass(pair, base + 3, base + 3, upward)

        def finish():
            self.z_other(pair, base + 3, upward)
            self.z_far(pair, base + 3)
            self.share(whole, base + 9)

        def done():
            self.arrive(whole(1 - core), base + 9)

        return [
            ("start", start),
            ("turn", turn),
            ("column", column),
            ("relay", relay),
            ("finish", finish),
            ("done", done),
        ]

    def late_steps(self, n):
        at, size = self.parts[n][1:]
        base = n * 19
        upward = n % 2 == 0
        x, y, z, core = self.x, self.y, self.z, self.core
        columns, local, slots = pl.ds(at, size), pl.ds(at - self.late_at, size), pl.ds(0, 2)
        shift = (x + n) % 4
        goal = (z + 8 - x - n % 4) % 4
        at_x = lambda step: (z + step + 8 - x - n % 4) % 4
        own = lambda step: self.late.at[0, at_x(step), :, local]
        passing = lambda step: self.late.at[1, at_x(step), :, local]
        piece = lambda slot, step: self.held.at[core, slot, at_x(step), :, columns]
        whole = lambda core: self.held.at[core, slots, :, :, columns]
        first, shifted = (self.moved.at[slot, :, columns] for slot in range(2))
        view = self.moved.at[jnp.where(shift == 0, 0, 1), :, columns]
        inner = jnp.where((y == 0) | (y == 2), 1, 2)
        slot = jnp.where((y == 0) | (y == 1), 1, 0)
        keep = pltpu.make_async_copy(
            self.late.at[0, :, :, local], self.held.at[core, y // 3, :, :, columns], self.sent.at[base + 17]
        )

        def start():
            self.send(first, shifted, base, base, device(x, y, (z + shift) % 4, core), shift != 0)

        def turn():
            pl.when(shift != 0)(lambda: self.arrive(shifted, base))
            target = self.late.at[0, x, :, local]
            self.send(view, target, base + 1, base + 1, device(goal, y, z, core), goal != x)
            pl.when(goal == x)(pltpu.make_async_copy(view, target, self.sent.at[base + 1]).start)

        def column():
            pl.when(goal == x)(pltpu.make_async_copy(view, own(0), self.sent.at[base + 1]).wait)
            pl.when(goal != x)(lambda: self.arrive(own(0), base + 1))
            self.z_start(own, base + 2, base + 2)

        def spread(step):
            sem = base + 5 + step
            self.send(own(step), passing(step), sem, base + 13 + step, device(x, 3 - y, z, core), self.edge)
            got = base + 5 + 4 * slot + step
            outer = device(x, y // 2 * 3, z, core)
            self.send(own(step), piece(slot, step), sem, got, outer, self.middle)
            self.send(own(step), piece(slot, step), sem + 4, got, device(x, inner, z, core), self.middle)

        def passed(step):
            pl.when(self.edge)(lambda: self.arrive(passing(step), base + 13 + step))
            got = base + 5 + 4 * slot + step
            self.send(passing(step), piece(slot, step), base + 9 + step, got, device(x, inner, z, core), self.edge)

        def relay():
            self.z_pass(own, base + 2, base + 2, upward)

        def second():
            self.z_other(own, base + 2, upward)
            spread(1 if upward else 3)

        def far():
            self.z_far(own, base + 2)
            spread(2)
            pl.when(self.edge)(keep.start)

        def finish():
            def arrived(slot):
                for step in range(4):
                    self.arrive(piece(slot, step), base + 5 + 4 * slot + step)

            def at_edge():
                arrived(1 - y // 3)
                keep.wait()

            def at_middle():
                arrived(0)
                arrived(1)

            pl.when(self.edge)(at_edge)
            pl.when(self.middle)(at_middle)
            self.share(whole, base + 18)

        def done():
            self.arrive(whole(1 - core), base + 18)

        near = 3 if upward else 1
        return [
            ("start", start),
            ("turn", turn),
            ("column", column),
            ("spread0", functools.partial(spread, 0)),
            ("relay", relay),
            ("spread1", functools.partial(spread, near)),
            ("second", second),
            ("far", far),
            ("passed0", functools.partial(passed, 0)),
            ("passed1", functools.partial(passed, near)),
            ("passed2", functools.partial(passed, 4 - near)),
            ("passed3", functools.partial(passed, 2)),
            ("finish", finish),
            ("done", done),
        ]

    def steps(self):
        steps = {}
        for n, part in enumerate(self.parts):
            made = (self.cross_steps, self.turn_steps, self.late_steps)[part[0]](n)
            steps.update({f"{n}.{name}": step for name, step in made})
        return steps

    def finish(self):
        for end in self.ends:
            end()


class Layer:
    def __init__(self, step_count, row_count, width, group, head, context):
        self.step_count, self.row_count, self.width = step_count, row_count, width
        self.group, self.head, self.context = group, head, context
        self.tokens = step_count * row_count
        self.share = width // 8

    def scratch(self):
        rows, context, head = self.row_count, self.context, self.head
        features = self.group * head
        return [
            pltpu.VMEM((self.width, features), BF),
            pltpu.VMEM((self.width, head), BF),
            pltpu.VMEM((self.width, head), BF),
            pltpu.VMEM((features, self.width), BF),
            pltpu.VMEM((rows, context, head), BF),
            pltpu.VMEM((rows, context, head), BF),
            pltpu.VMEM((8, self.tokens, self.share), F32),
            pltpu.VMEM((8, self.tokens, self.share), F32),
            pltpu.VMEM((8, self.tokens, self.share), F32),
            pltpu.SemaphoreType.DMA((5 + 2 * rows,)),
            pltpu.SemaphoreType.DMA((14,)),
            pltpu.SemaphoreType.DMA((16,)),
        ]

    def begin(self, hidden, lengths, gain, sources, mixed, scratch):
        self.hidden, self.lengths, self.gain = hidden, lengths, gain
        self.w_query, self.w_key, self.w_value, self.w_out = scratch[:4]
        self.keys, self.values, self.partial, self.landed, self.mixed = scratch[4:9]
        loads, self.sent, self.got = scratch[9:]
        self.result = pltpu.make_async_copy(self.mixed, mixed, loads.at[4 + 2 * self.row_count])
        w_query, w_key, w_value, w_out, keys, values = sources
        pairs = [(w_query, self.w_query), (w_key, self.w_key), (w_value, self.w_value)]
        for r in range(self.row_count):
            pairs.append((keys.at[r, 0], self.keys.at[r]))
            pairs.append((values.at[r, 0], self.values.at[r]))
        pairs.append((w_out, self.w_out))
        self.loads = [pltpu.make_async_copy(a, b, loads.at[i]) for i, (a, b) in enumerate(pairs)]
        for load in self.loads:
            load.start()
        self.ends = []
        self.rows = {}

    def normalize(self):
        values = jnp.concatenate([self.hidden[s] for s in range(self.step_count)], axis=0).astype(F32)
        scale = lax.rsqrt(jnp.mean(values * values, axis=-1, keepdims=True) + 1e-06)
        self.normed = (values * scale * self.gain[...]).astype(BF)

    def turn(self):
        steps, rows, half = self.step_count, self.row_count, self.head // 2
        token = lax.broadcasted_iota(jnp.int32, (self.tokens, self.head), 0)
        lane = lax.broadcasted_iota(jnp.int32, (self.tokens, self.head), 1)
        position = token // rows
        for r in range(rows):
            position = position + jnp.where(token % rows == r, self.lengths[r], 0)
        power = (lane % half).astype(F32) * (2.0 / self.head)
        angles = position.astype(F32) * jnp.exp(-power * math.log(1000000.0))
        self.cosine = jnp.cos(angles)
        sine = jnp.sin(angles)
        self.sine = jnp.where(lane < half, -sine, sine)

    def rotate(self, vectors):
        return (vectors * self.cosine + pltpu.roll(vectors, self.head // 2, 1) * self.sine).astype(BF)

    def project_query(self, g):
        if g == 0:
            self.loads[0].wait()
            self.query = []
        at = g * self.head
        wide = jnp.dot(self.normed, self.w_query[:, at : at + self.head], preferred_element_type=F32)
        self.query.append(self.rotate(wide))

    def project_query_pair(self, g):
        if g == 0:
            self.loads[0].wait()
            self.query = []
        at = g * self.head
        wide = jnp.dot(self.normed, self.w_query[:, at : at + 2 * self.head], preferred_element_type=F32)
        self.query.append(self.rotate(wide[:, : self.head]))
        self.query.append(self.rotate(wide[:, self.head :]))

    def project_key(self):
        self.loads[1].wait()
        self.fresh_key = self.rotate(jnp.dot(self.normed, self.w_key[...], preferred_element_type=F32))

    def project_value(self):
        self.loads[2].wait()
        self.fresh_value = jnp.dot(self.normed, self.w_value[...], preferred_element_type=F32).astype(BF)

    def pick(self, size, total, test):
        out = lax.broadcasted_iota(jnp.int32, (size, total), 0)
        inner = lax.broadcasted_iota(jnp.int32, (size, total), 1)
        return test(out, inner).astype(F32).astype(BF)

    def score(self, r):
        self.loads[3 + 2 * r].wait()
        steps, rows, tokens = self.step_count, self.row_count, self.tokens
        heads = self.group * steps
        every = jnp.concatenate(self.query, axis=0)
        chosen = self.pick(
            heads, self.group * tokens, lambda o, i: i == (o // steps) * tokens + (o % steps) * rows + r
        )
        query = jnp.dot(chosen, every, preferred_element_type=F32).astype(BF)
        scale = 1.0 / math.sqrt(self.head)
        along = (((1,), (1,)), ((), ()))
        cached = lax.dot_general(query, self.keys[r], along, preferred_element_type=F32) * scale
        slot = lax.broadcasted_iota(jnp.int32, cached.shape, 1)
        cached = jnp.where(slot < self.lengths[r], cached, -jnp.inf)
        recent = lax.dot_general(query, self.fresh_key, along, preferred_element_type=F32) * scale
        out = lax.broadcasted_iota(jnp.int32, recent.shape, 0)
        token = lax.broadcasted_iota(jnp.int32, recent.shape, 1)
        recent = jnp.where((token % rows == r) & (token // rows <= out % steps), recent, -jnp.inf)
        top = jnp.maximum(
            jnp.max(cached, axis=-1, keepdims=True), jnp.max(recent, axis=-1, keepdims=True)
        )
        cached_exp = jnp.exp(cached - top)
        recent_exp = jnp.exp(recent - top)
        total = jnp.sum(cached_exp, axis=-1, keepdims=True) + jnp.sum(recent_exp, axis=-1, keepdims=True)
        self.rows[r] = (cached_exp / total).astype(BF), (recent_exp / total).astype(BF)

    def attend(self, r):
        self.loads[4 + 2 * r].wait()
        cached, recent = self.rows[r]
        result = jnp.dot(cached, self.values[r], preferred_element_type=F32)
        result = result + jnp.dot(recent, self.fresh_value, preferred_element_type=F32)
        self.rows[r] = result.astype(BF)

    def lay_out(self):
        steps, rows, tokens = self.step_count, self.row_count, self.tokens
        heads = self.group * steps
        every = jnp.concatenate([self.rows[r] for r in range(rows)], axis=0)
        parts = []
        for g in range(self.group):
            chosen = self.pick(
                tokens, rows * heads, lambda o, i: i == (o % rows) * heads + g * steps + o // rows
            )
            parts.append(jnp.dot(chosen, every, preferred_element_type=F32).astype(BF))
        self.attended = jnp.concatenate(parts, axis=1)

    def project_out(self, t):
        if t == 0:
            self.loads[-1].wait()
        columns = slice(t * self.share, (t + 1) * self.share)
        self.partial[t] = jnp.dot(self.attended, self.w_out[:, columns], preferred_element_type=F32)

    def group_peers(self):
        dp, tp = lax.axis_index("dp"), lax.axis_index("tp")
        return [(dp, (tp + step) % 8) for step in range(1, 8)]

    def copy(self, source, target, sent, got, to):
        return pltpu.make_async_remote_copy(
            src_ref=source,
            dst_ref=target,
            send_sem=self.sent.at[sent],
            recv_sem=self.got.at[got],
            device_id=to,
            device_id_type=MESH,
        )

    def scatter(self):
        me = lax.axis_index("tp")
        for step, peer in enumerate(self.group_peers(), 1):
            copy = self.copy(self.partial.at[peer[1]], self.landed.at[step], step - 1, step, peer)
            copy.start()
            self.ends.append(copy.wait_send)

    def gather(self):
        me = lax.axis_index("tp")
        total = self.partial[me]
        for step, peer in enumerate(self.group_peers(), 1):
            self.copy(self.landed.at[step], self.landed.at[step], 0, step, peer).wait_recv()
            total = total + self.landed[step]
        self.mixed[me] = total
        for step, peer in enumerate(self.group_peers(), 1):
            copy = self.copy(self.mixed.at[me], self.mixed.at[me], 6 + step, 8 + step, peer)
            copy.start()
            self.ends.append(copy.wait_send)

    def collect(self):
        me = lax.axis_index("tp")
        for step, peer in enumerate(self.group_peers(), 1):
            owner = (me + 8 - step) % 8
            self.copy(self.mixed.at[owner], self.mixed.at[owner], 0, 8 + step, peer).wait_recv()
        self.result.start()
        self.ends.append(self.result.wait)

    def steps(self):
        steps = {"normalize": self.normalize, "turn": self.turn}
        for g in range(0, self.group, 2):
            steps[f"query{g}"] = functools.partial(self.project_query_pair, g)
        steps["key"] = self.project_key
        steps["value"] = self.project_value
        for r in range(self.row_count):
            steps[f"score{r}"] = functools.partial(self.score, r)
            steps[f"attend{r}"] = functools.partial(self.attend, r)
        steps["lay_out"] = self.lay_out
        for t in range(8):
            steps[f"out{t}"] = functools.partial(self.project_out, t)
        steps["scatter"] = self.scatter
        steps["gather"] = self.gather
        steps["collect"] = self.collect
        return steps

    def finish(self):
        for end in self.ends:
            end()


def kernel(gather, layer, *refs):
    lengths, hidden, gain, q, k, v = refs[:6]
    sources, (held, mixed) = refs[6:12], refs[12:14]
    moved, ring, late, small, sent, got, own, hidden_here, gain_here, lengths_here = refs[14:24]
    gather.begin(held, moved, ring, late, sent, got)
    high, low = q.shape[0], k.shape[0]
    pairs = [
        (q, moved.at[0, pl.ds(0, high), :]),
        (k, small.at[0]),
        (v, small.at[1]),
        (hidden, hidden_here),
        (gain, gain_here),
        (lengths, lengths_here),
    ]
    loads = [pltpu.make_async_copy(a, b, own.at[i]) for i, (a, b) in enumerate(pairs)]
    for load in loads:
        load.start()
    layer.begin(hidden_here, lengths_here, gain_here, sources, mixed, refs[24:])
    gather.greet(loads)
    moved[0, pl.ds(high, 2 * low), :] = jnp.concatenate([small[0], small[1]], axis=0)
    steps = [*gather.steps().values(), *layer.steps().values()]
    for number in ORDER:
        steps[number]()
    gather.finish()
    layer.finish()


def write_out(held, mixed, q, k, v, out, low_k, low_v, sems):
    high, low = q.shape[3], k.shape[2] // 4
    copies = [pltpu.make_async_copy(held.at[:, :, :, pl.ds(0, high), :], q, sems.at[0])]
    copies[0].start()
    for core in range(2):
        for slot in range(2):
            for at, (staged, target) in enumerate(((low_k, k), (low_v, v))):
                rows = slice(high + at * low, high + (at + 1) * low)
                staged[core, slot] = jnp.concatenate([held[core, slot, x, rows, :] for x in range(4)], axis=0)
                part = (core, slot)
                copies.append(pltpu.make_async_copy(staged.at[part], target.at[part], sems.at[len(copies)]))
                copies[-1].start()
    steps, rows, _ = out.shape
    share = mixed.shape[2]
    for t in range(mixed.shape[0]):
        for s in range(steps):
            out[s, :, t * share : (t + 1) * share] = mixed[t, s * rows : (s + 1) * rows, :].astype(BF)
    for copy in copies:
        copy.wait()


def on_device(
    hidden,
    lengths,
    norm_gain,
    w_query,
    key_weight_matrix,
    value_weight_matrix,
    w_out,
    key_cache,
    cached_value_rows,
    next_query,
    upcoming_key_weight,
    upcoming_value_weight,
):
    step_count, row_count, width = hidden.shape
    head = key_cache.shape[3]
    group = w_query.shape[1] // head
    context = key_cache.shape[2]
    tokens = step_count * row_count
    high, low = next_query.shape[0], upcoming_key_weight.shape[0]
    rows = high + 2 * low
    gather = Gather(rows, width)
    layer = Layer(step_count, row_count, width, group, head, context)
    vmem = pl.BlockSpec(memory_space=pltpu.VMEM)
    hbm = pl.BlockSpec(memory_space=pltpu.HBM)
    held, mixed = pl.pallas_call(
        functools.partial(kernel, gather, layer),
        out_shape=(
            jax.ShapeDtypeStruct((2, 2, 4, rows, width), BF),
            jax.ShapeDtypeStruct((8, tokens, width // 8), F32),
        ),
        in_specs=[hbm] * 12,
        out_specs=(pl.BlockSpec(memory_space=pl.ANY),) * 2,
        scratch_shapes=[
            *gather.scratch()[:3],
            pltpu.VMEM((2, low, width), BF),
            *gather.scratch()[3:],
            pltpu.SemaphoreType.DMA((6,)),
            pltpu.VMEM((step_count, row_count, width), BF),
            pltpu.VMEM((1, width), F32),
            pltpu.SMEM((row_count,), jnp.int32),
            *layer.scratch(),
        ],
        compiler_params=pltpu.CompilerParams(
            collective_id=0, has_side_effects=True, vmem_limit_bytes=VMEM_LIMIT
        ),
        cost_estimate=pl.CostEstimate(flops=10**9, bytes_accessed=40 * 2**20, transcendentals=10**5),
    )(
        *(
            pltpu.with_memory_space_constraint(each, pltpu.HBM)
            for each in (
                lengths,
                hidden,
                norm_gain.reshape(1, width),
                next_query,
                upcoming_key_weight,
                upcoming_value_weight,
                w_query,
                key_weight_matrix,
                value_weight_matrix,
                w_out,
                key_cache,
                cached_value_rows,
            )
        ),
    )
    q, k, v, mixed = pl.pallas_call(
        write_out,
        out_shape=(
            jax.ShapeDtypeStruct((2, 2, 4, high, width), BF),
            jax.ShapeDtypeStruct((2, 2, 4 * low, width), BF),
            jax.ShapeDtypeStruct((2, 2, 4 * low, width), BF),
            jax.ShapeDtypeStruct((step_count, row_count, width), BF),
        ),
        in_specs=[vmem] * 2,
        out_specs=(hbm, hbm, hbm, vmem),
        scratch_shapes=[
            pltpu.VMEM((2, 2, 4 * low, width), BF),
            pltpu.VMEM((2, 2, 4 * low, width), BF),
            pltpu.SemaphoreType.DMA((9,)),
        ],
        compiler_params=pltpu.CompilerParams(vmem_limit_bytes=16 * 2**20),
    )(
        pltpu.with_memory_space_constraint(held, pltpu.VMEM),
        pltpu.with_memory_space_constraint(mixed, pltpu.VMEM),
    )
    return mixed, q.reshape(-1, width), k.reshape(-1, width), v.reshape(-1, width)


def solution(mesh):
    in_specs = (
        P(None, "dp", None),
        P("dp"),
        P(),
        P(None, "tp"),
        P(None, "tp"),
        P(None, "tp"),
        P("tp", None),
        P("dp", "tp", None, None),
        P("dp", "tp", None, None),
        P(("dp", "tp"), None),
        P(("dp", "tp"), None),
        P(("dp", "tp"), None),
    )
    out_specs = (P(None, "dp", None), P("tp", None), P("tp", None), P("tp", None))
    return jax.shard_map(
        on_device, mesh=mesh, in_specs=in_specs, out_specs=out_specs, check_vma=False
    )
```

```python
import functools
import math

import jax
import jax.numpy as jnp
from jax import lax
from jax.experimental import pallas as pl
from jax.experimental.pallas import tpu as pltpu
from jax.sharding import PartitionSpec as P

MESH = pl.DeviceIdType.MESH
BF = jnp.bfloat16
F32 = jnp.float32

CROSS = 640
TURN = 2432
CROSS_PARTS = 2
TURN_PARTS = 4
LATE_PARTS = 3
VMEM_LIMIT = 36 * 2**20
ORDER = (
    42, 0, 56, 9, 70, 18, 43, 84, 85, 24, 57, 86, 1, 30, 2, 44, 87, 45, 71, 10, 19, 36, 11, 58, 88, 89, 59,
    3, 4, 5, 25, 90, 46, 72, 91, 47, 73, 48, 50, 92, 12, 93, 20, 13, 94, 95, 14, 31, 60, 96, 61, 62, 64, 26,
    97, 98, 99, 37, 49, 100, 74, 75, 76, 51, 52, 78, 101, 6, 32, 102, 103, 104, 21, 63, 65, 66, 105, 15, 38,
    106, 107, 27, 77, 79, 80, 53, 7, 33, 67, 16, 22, 108, 39, 54, 81, 28, 68, 34, 82, 40, 109, 8, 17, 23, 29,
    35, 41, 55, 69, 83,
)


def place():
    dp, tp = lax.axis_index("dp"), lax.axis_index("tp")
    return tp % 4, (dp // 8) * 2 + tp // 4, (dp // 2) % 4, dp % 2


def device(x, y, z, core):
    return ((y // 2) * 8 + z * 2 + core, (y % 2) * 4 + x)


def cut(start, width, parts):
    tiles = width // 128
    edges = [128 * (tiles * i // parts) for i in range(parts + 1)]
    return [(start + edges[i], edges[i + 1] - edges[i]) for i in range(parts)]


class Gather:
    def __init__(self, rows, width):
        self.rows, self.width = rows, width
        bounds = [(0, CROSS, CROSS_PARTS), (CROSS, TURN, TURN_PARTS)]
        self.late_at = CROSS + TURN
        bounds.append((self.late_at, width - self.late_at, LATE_PARTS))
        self.parts = [(kind, at, size) for kind, bound in enumerate(bounds) for at, size in cut(*bound)]
        self.count = len(self.parts) * 19

    def scratch(self):
        return [
            pltpu.VMEM((2, self.rows, self.width), BF),
            pltpu.VMEM((4, 2, self.rows, CROSS), BF),
            pltpu.VMEM((2, 4, self.rows, self.width - self.late_at), BF),
            pltpu.SemaphoreType.DMA((self.count,)),
            pltpu.SemaphoreType.DMA((self.count,)),
        ]

    def begin(self, held, moved, ring, late, sent, got):
        self.held, self.moved, self.ring, self.late, self.sent, self.got = held, moved, ring, late, sent, got
        self.x, self.y, self.z, self.core = place()
        self.edge = (self.y == 0) | (self.y == 3)
        self.middle = jnp.logical_not(self.edge)
        self.ends = []

    def greet(self):
        x, y, z, core = self.x, self.y, self.z, self.core
        barrier = pltpu.get_barrier_semaphore()

        def signal(peers):
            for peer in peers:
                pl.semaphore_signal(barrier, inc=1, device_id=peer, device_id_type=MESH)

        def row(at_y, first=0):
            return [device((x + i) % 4, at_y, z, core) for i in range(first, 4)]

        signal([device(x, y, (z + i) % 4, core) for i in range(1, 4)] + [device(x, y, z, 1 - core)])
        signal(row(y, 1) + row(y // 2 * 2 + 1 - y % 2))
        pl.when(self.edge)(lambda: signal([device(x, 3 - y, z, core)]))
        pl.when(self.middle)(lambda: signal(row(y % 2 * 2) + row(y % 2 * 2 + 1)))

    def meet(self, loads):
        for load in loads:
            load.wait()
        pl.semaphore_wait(pltpu.get_barrier_semaphore(), 15 + self.edge.astype(jnp.int32))

    def send(self, source, target, sent, got, to, when=None):
        copy = pltpu.make_async_remote_copy(
            src_ref=source,
            dst_ref=target,
            send_sem=self.sent.at[sent],
            recv_sem=self.got.at[got],
            device_id=to,
            device_id_type=MESH,
        )
        if when is None:
            copy.start()
            self.ends.append(copy.wait_send)
        else:
            pl.when(when)(copy.start)
            self.ends.append(lambda: pl.when(when)(copy.wait_send))

    def arrive(self, target, got):
        pltpu.make_async_remote_copy(
            src_ref=target,
            dst_ref=target,
            send_sem=self.sent.at[0],
            recv_sem=self.got.at[got],
            device_id=device(self.x, self.y, self.z, 1 - self.core),
            device_id_type=MESH,
        ).wait_recv()

    def z_start(self, view, sent, got):
        own = view(0)
        self.send(own, own, sent, got, device(self.x, self.y, (self.z + 1) % 4, self.core))
        self.send(own, own, sent + 1, got + 1, device(self.x, self.y, (self.z + 3) % 4, self.core))

    def z_pass(self, view, sent, got, upward):
        near, step = (3, 1) if upward else (1, 3)
        piece = view(near)
        self.arrive(piece, got + (0 if upward else 1))
        self.send(piece, piece, sent + 2, got + 2, device(self.x, self.y, (self.z + step) % 4, self.core))

    def z_other(self, view, got, upward):
        self.arrive(view(1 if upward else 3), got + (1 if upward else 0))

    def z_far(self, view, got):
        self.arrive(view(2), got + 2)

    def both(self, view, target, sent, got, x, stays):
        y = self.y
        for which in range(2):
            goal_y = y // 2 + 2 * which
            here = stays & (goal_y == y)
            self.send(view, target, sent + which, got + y % 2, device(x, goal_y, self.z, self.core), jnp.logical_not(here))
            pl.when(here)(pltpu.make_async_copy(view, target, self.sent.at[sent + which]).start)

    def land(self, view, target, slot, sent, got, stays):
        y = self.y
        here = stays & (y % 2 * 2 + slot == y)
        pl.when(here)(pltpu.make_async_copy(view, target, self.sent.at[sent + y // 2]).wait)
        pl.when(jnp.logical_not(here))(lambda: self.arrive(target, got + slot))

    def share(self, whole, sem):
        self.send(whole(self.core), whole(self.core), sem, sem, device(self.x, self.y, self.z, 1 - self.core))

    def cross_steps(self, n):
        at, size = self.parts[n][1:]
        base = n * 19
        upward = n % 2 == 0
        x, y, z, core = self.x, self.y, self.z, self.core
        columns, slots = pl.ds(at, size), pl.ds(0, 2)
        here = jnp.bool_(True)
        first = self.moved.at[0, :, columns]
        view = lambda step: self.ring.at[(z + step) % 4, :, :, columns]
        at_z = lambda to_x: self.ring.at[to_x, :, :, columns]
        final = lambda from_x: self.held.at[core, slots, from_x, :, columns]
        whole = lambda core: self.held.at[core, slots, :, :, columns]

        def start():
            self.both(first, self.ring.at[z, y % 2, :, columns], base, base, x, here)

        def column():
            for slot in range(2):
                self.land(first, self.ring.at[z, slot, :, columns], slot, base, base, here)
            self.z_start(view, base + 2, base + 2)

        def cross(step):
            goal = (z + step) % 4
            hops = (goal - x + 4) % 4
            to = device(goal, y, z, core)
            self.send(at_z(goal), final(x), base + 5 + step, base + 4 + hops, to, hops != 0)
            stay = pltpu.make_async_copy(at_z(goal), final(x), self.sent.at[base + 5 + step])
            pl.when(hops == 0)(stay.start)

        def relay():
            self.z_pass(view, base + 2, base + 2, upward)

        def second():
            self.z_other(view, base + 2, upward)
            cross(1 if upward else 3)

        def far():
            self.z_far(view, base + 2)
            cross(2)

        def finish():
            step = (x - z + 4) % 4
            pltpu.make_async_copy(at_z(x), final(x), self.sent.at[base + 5 + step]).wait()
            for hops in range(1, 4):
                self.arrive(final((x + 4 - hops) % 4), base + 4 + hops)
            self.share(whole, base + 9)

        def done():
            self.arrive(whole(1 - core), base + 9)

        return [
            ("start", start),
            ("column", column),
            ("cross0", functools.partial(cross, 0)),
            ("relay", relay),
            ("cross1", functools.partial(cross, 3 if upward else 1)),
            ("second", second),
            ("far", far),
            ("finish", finish),
            ("done", done),
        ]

    def turn_steps(self, n):
        at, size = self.parts[n][1:]
        base = n * 19
        upward = n % 2 == 0
        x, y, z, core = self.x, self.y, self.z, self.core
        columns, slots = pl.ds(at, size), pl.ds(0, 2)
        shift = (x + n) % 4
        goal = (z + 8 - x - n % 4) % 4
        at_x = lambda step: (z + step + 8 - x - n % 4) % 4
        pair = lambda step: self.held.at[core, slots, at_x(step), :, columns]
        whole = lambda core: self.held.at[core, slots, :, :, columns]
        first, shifted = (self.moved.at[slot, :, columns] for slot in range(2))
        view = self.moved.at[jnp.where(shift == 0, 0, 1), :, columns]

        def start():
            self.send(first, shifted, base, base, device(x, y, (z + shift) % 4, core), shift != 0)

        def turn():
            pl.when(shift != 0)(lambda: self.arrive(shifted, base))
            self.both(view, self.held.at[core, y % 2, x, :, columns], base + 1, base + 1, goal, goal == x)

        def column():
            for slot in range(2):
                target = self.held.at[core, slot, at_x(0), :, columns]
                self.land(view, target, slot, base + 1, base + 1, at_x(0) == x)
            self.z_start(pair, base + 3, base + 3)

        def relay():
            self.z_pass(pair, base + 3, base + 3, upward)

        def finish():
            self.z_other(pair, base + 3, upward)
            self.z_far(pair, base + 3)
            self.share(whole, base + 9)

        def done():
            self.arrive(whole(1 - core), base + 9)

        return [
            ("start", start),
            ("turn", turn),
            ("column", column),
            ("relay", relay),
            ("finish", finish),
            ("done", done),
        ]

    def late_steps(self, n):
        at, size = self.parts[n][1:]
        base = n * 19
        upward = n % 2 == 0
        x, y, z, core = self.x, self.y, self.z, self.core
        columns, local, slots = pl.ds(at, size), pl.ds(at - self.late_at, size), pl.ds(0, 2)
        shift = (x + n) % 4
        goal = (z + 8 - x - n % 4) % 4
        at_x = lambda step: (z + step + 8 - x - n % 4) % 4
        own = lambda step: self.late.at[0, at_x(step), :, local]
        passing = lambda step: self.late.at[1, at_x(step), :, local]
        piece = lambda slot, step: self.held.at[core, slot, at_x(step), :, columns]
        whole = lambda core: self.held.at[core, slots, :, :, columns]
        first, shifted = (self.moved.at[slot, :, columns] for slot in range(2))
        view = self.moved.at[jnp.where(shift == 0, 0, 1), :, columns]
        inner = jnp.where((y == 0) | (y == 2), 1, 2)
        slot = jnp.where((y == 0) | (y == 1), 1, 0)
        keep = pltpu.make_async_copy(
            self.late.at[0, :, :, local], self.held.at[core, y // 3, :, :, columns], self.sent.at[base + 17]
        )

        def start():
            self.send(first, shifted, base, base, device(x, y, (z + shift) % 4, core), shift != 0)

        def turn():
            pl.when(shift != 0)(lambda: self.arrive(shifted, base))
            target = self.late.at[0, x, :, local]
            self.send(view, target, base + 1, base + 1, device(goal, y, z, core), goal != x)
            pl.when(goal == x)(pltpu.make_async_copy(view, target, self.sent.at[base + 1]).start)

        def column():
            pl.when(goal == x)(pltpu.make_async_copy(view, own(0), self.sent.at[base + 1]).wait)
            pl.when(goal != x)(lambda: self.arrive(own(0), base + 1))
            self.z_start(own, base + 2, base + 2)

        def spread(step):
            sem = base + 5 + step
            self.send(own(step), passing(step), sem, base + 13 + step, device(x, 3 - y, z, core), self.edge)
            got = base + 5 + 4 * slot + step
            outer = device(x, y // 2 * 3, z, core)
            self.send(own(step), piece(slot, step), sem, got, outer, self.middle)
            self.send(own(step), piece(slot, step), sem + 4, got, device(x, inner, z, core), self.middle)

        def passed(step):
            pl.when(self.edge)(lambda: self.arrive(passing(step), base + 13 + step))
            got = base + 5 + 4 * slot + step
            self.send(passing(step), piece(slot, step), base + 9 + step, got, device(x, inner, z, core), self.edge)

        def relay():
            self.z_pass(own, base + 2, base + 2, upward)

        def second():
            self.z_other(own, base + 2, upward)
            spread(1 if upward else 3)

        def far():
            self.z_far(own, base + 2)
            spread(2)
            pl.when(self.edge)(keep.start)

        def finish():
            def arrived(slot):
                for step in range(4):
                    self.arrive(piece(slot, step), base + 5 + 4 * slot + step)

            def at_edge():
                arrived(1 - y // 3)
                keep.wait()

            def at_middle():
                arrived(0)
                arrived(1)

            pl.when(self.edge)(at_edge)
            pl.when(self.middle)(at_middle)
            self.share(whole, base + 18)

        def done():
            self.arrive(whole(1 - core), base + 18)

        near = 3 if upward else 1
        return [
            ("start", start),
            ("turn", turn),
            ("column", column),
            ("spread0", functools.partial(spread, 0)),
            ("relay", relay),
            ("spread1", functools.partial(spread, near)),
            ("second", second),
            ("far", far),
            ("passed0", functools.partial(passed, 0)),
            ("passed1", functools.partial(passed, near)),
            ("passed2", functools.partial(passed, 4 - near)),
            ("passed3", functools.partial(passed, 2)),
            ("finish", finish),
            ("done", done),
        ]

    def steps(self):
        steps = {}
        for n, part in enumerate(self.parts):
            made = (self.cross_steps, self.turn_steps, self.late_steps)[part[0]](n)
            steps.update({f"{n}.{name}": step for name, step in made})
        return steps

    def finish(self):
        for end in self.ends:
            end()


class Layer:
    def __init__(self, step_count, row_count, width, group, head, context):
        self.step_count, self.row_count, self.width = step_count, row_count, width
        self.group, self.head, self.context = group, head, context
        self.tokens = step_count * row_count
        self.share = width // 8

    def scratch(self):
        rows, context, head = self.row_count, self.context, self.head
        features = self.group * head
        return [
            pltpu.VMEM((self.width, features), BF),
            pltpu.VMEM((self.width, head), BF),
            pltpu.VMEM((self.width, head), BF),
            pltpu.VMEM((features, self.width), BF),
            pltpu.VMEM((rows, context, head), BF),
            pltpu.VMEM((rows, context, head), BF),
            pltpu.VMEM((8, self.tokens, self.share), F32),
            pltpu.VMEM((8, self.tokens, self.share), F32),
            pltpu.VMEM((8, self.tokens, self.share), F32),
            pltpu.SemaphoreType.DMA((5 + 2 * rows,)),
            pltpu.SemaphoreType.DMA((14,)),
            pltpu.SemaphoreType.DMA((16,)),
        ]

    def begin(self, hidden, lengths, gain, sources, mixed, scratch):
        self.hidden, self.lengths, self.gain = hidden, lengths, gain
        self.w_query, self.w_key, self.w_value, self.w_out = scratch[:4]
        self.keys, self.values, self.partial, self.landed, self.mixed = scratch[4:9]
        loads, self.sent, self.got = scratch[9:]
        self.result = pltpu.make_async_copy(self.mixed, mixed, loads.at[4 + 2 * self.row_count])
        w_query, w_key, w_value, w_out, keys, values = sources
        pairs = [(w_query, self.w_query), (w_key, self.w_key), (w_value, self.w_value)]
        for r in range(self.row_count):
            pairs.append((keys.at[r, 0], self.keys.at[r]))
            pairs.append((values.at[r, 0], self.values.at[r]))
        pairs.append((w_out, self.w_out))
        self.loads = [pltpu.make_async_copy(a, b, loads.at[i]) for i, (a, b) in enumerate(pairs)]
        for load in self.loads:
            load.start()
        self.ends = []
        self.rows = {}

    def normalize(self):
        values = jnp.concatenate([self.hidden[s] for s in range(self.step_count)], axis=0).astype(F32)
        scale = lax.rsqrt(jnp.mean(values * values, axis=-1, keepdims=True) + 1e-06)
        self.normed = (values * scale * self.gain[...]).astype(BF)

    def turn(self):
        steps, rows, half = self.step_count, self.row_count, self.head // 2
        token = lax.broadcasted_iota(jnp.int32, (self.tokens, self.head), 0)
        lane = lax.broadcasted_iota(jnp.int32, (self.tokens, self.head), 1)
        position = token // rows
        for r in range(rows):
            position = position + jnp.where(token % rows == r, self.lengths[r], 0)
        power = (lane % half).astype(F32) * (2.0 / self.head)
        angles = position.astype(F32) * jnp.exp(-power * math.log(1000000.0))
        self.cosine = jnp.cos(angles)
        sine = jnp.sin(angles)
        self.sine = jnp.where(lane < half, -sine, sine)

    def rotate(self, vectors):
        return (vectors * self.cosine + pltpu.roll(vectors, self.head // 2, 1) * self.sine).astype(BF)

    def project_query(self, g):
        if g == 0:
            self.loads[0].wait()
            self.query = []
        at = g * self.head
        wide = jnp.dot(self.normed, self.w_query[:, at : at + self.head], preferred_element_type=F32)
        self.query.append(self.rotate(wide))

    def project_query_pair(self, g):
        if g == 0:
            self.loads[0].wait()
            self.query = []
        at = g * self.head
        wide = jnp.dot(self.normed, self.w_query[:, at : at + 2 * self.head], preferred_element_type=F32)
        self.query.append(self.rotate(wide[:, : self.head]))
        self.query.append(self.rotate(wide[:, self.head :]))

    def project_key(self):
        self.loads[1].wait()
        self.fresh_key = self.rotate(jnp.dot(self.normed, self.w_key[...], preferred_element_type=F32))

    def project_value(self):
        self.loads[2].wait()
        self.fresh_value = jnp.dot(self.normed, self.w_value[...], preferred_element_type=F32).astype(BF)

    def pick(self, size, total, test):
        out = lax.broadcasted_iota(jnp.int32, (size, total), 0)
        inner = lax.broadcasted_iota(jnp.int32, (size, total), 1)
        return test(out, inner).astype(F32).astype(BF)

    def score(self, r):
        self.loads[3 + 2 * r].wait()
        steps, rows, tokens = self.step_count, self.row_count, self.tokens
        heads = self.group * steps
        every = jnp.concatenate(self.query, axis=0)
        chosen = self.pick(
            heads, self.group * tokens, lambda o, i: i == (o // steps) * tokens + (o % steps) * rows + r
        )
        query = jnp.dot(chosen, every, preferred_element_type=F32).astype(BF)
        scale = 1.0 / math.sqrt(self.head)
        along = (((1,), (1,)), ((), ()))
        cached = lax.dot_general(query, self.keys[r], along, preferred_element_type=F32) * scale
        slot = lax.broadcasted_iota(jnp.int32, cached.shape, 1)
        cached = jnp.where(slot < self.lengths[r], cached, -jnp.inf)
        recent = lax.dot_general(query, self.fresh_key, along, preferred_element_type=F32) * scale
        out = lax.broadcasted_iota(jnp.int32, recent.shape, 0)
        token = lax.broadcasted_iota(jnp.int32, recent.shape, 1)
        recent = jnp.where((token % rows == r) & (token // rows <= out % steps), recent, -jnp.inf)
        top = jnp.maximum(
            jnp.max(cached, axis=-1, keepdims=True), jnp.max(recent, axis=-1, keepdims=True)
        )
        cached_exp = jnp.exp(cached - top)
        recent_exp = jnp.exp(recent - top)
        total = jnp.sum(cached_exp, axis=-1, keepdims=True) + jnp.sum(recent_exp, axis=-1, keepdims=True)
        self.rows[r] = (cached_exp / total).astype(BF), (recent_exp / total).astype(BF)

    def attend(self, r):
        self.loads[4 + 2 * r].wait()
        cached, recent = self.rows[r]
        result = jnp.dot(cached, self.values[r], preferred_element_type=F32)
        result = result + jnp.dot(recent, self.fresh_value, preferred_element_type=F32)
        self.rows[r] = result.astype(BF)

    def lay_out(self):
        steps, rows, tokens = self.step_count, self.row_count, self.tokens
        heads = self.group * steps
        every = jnp.concatenate([self.rows[r] for r in range(rows)], axis=0)
        parts = []
        for g in range(self.group):
            chosen = self.pick(
                tokens, rows * heads, lambda o, i: i == (o % rows) * heads + g * steps + o // rows
            )
            parts.append(jnp.dot(chosen, every, preferred_element_type=F32).astype(BF))
        self.attended = jnp.concatenate(parts, axis=1)

    def project_out(self, t):
        if t == 0:
            self.loads[-1].wait()
        columns = slice(t * self.share, (t + 1) * self.share)
        self.partial[t] = jnp.dot(self.attended, self.w_out[:, columns], preferred_element_type=F32)

    def group_peers(self):
        dp, tp = lax.axis_index("dp"), lax.axis_index("tp")
        return [(dp, (tp + step) % 8) for step in range(1, 8)]

    def copy(self, source, target, sent, got, to):
        return pltpu.make_async_remote_copy(
            src_ref=source,
            dst_ref=target,
            send_sem=self.sent.at[sent],
            recv_sem=self.got.at[got],
            device_id=to,
            device_id_type=MESH,
        )

    def scatter(self):
        me = lax.axis_index("tp")
        for step, peer in enumerate(self.group_peers(), 1):
            copy = self.copy(self.partial.at[peer[1]], self.landed.at[step], step - 1, step, peer)
            copy.start()
            self.ends.append(copy.wait_send)

    def gather(self):
        me = lax.axis_index("tp")
        total = self.partial[me]
        for step, peer in enumerate(self.group_peers(), 1):
            self.copy(self.landed.at[step], self.landed.at[step], 0, step, peer).wait_recv()
            total = total + self.landed[step]
        self.mixed[me] = total
        for step, peer in enumerate(self.group_peers(), 1):
            copy = self.copy(self.mixed.at[me], self.mixed.at[me], 6 + step, 8 + step, peer)
            copy.start()
            self.ends.append(copy.wait_send)

    def collect(self):
        me = lax.axis_index("tp")
        for step, peer in enumerate(self.group_peers(), 1):
            owner = (me + 8 - step) % 8
            self.copy(self.mixed.at[owner], self.mixed.at[owner], 0, 8 + step, peer).wait_recv()
        self.result.start()
        self.ends.append(self.result.wait)

    def steps(self):
        steps = {"normalize": self.normalize, "turn": self.turn}
        for g in range(0, self.group, 2):
            steps[f"query{g}"] = functools.partial(self.project_query_pair, g)
        steps["key"] = self.project_key
        steps["value"] = self.project_value
        for r in range(self.row_count):
            steps[f"score{r}"] = functools.partial(self.score, r)
            steps[f"attend{r}"] = functools.partial(self.attend, r)
        steps["lay_out"] = self.lay_out
        for t in range(8):
            steps[f"out{t}"] = functools.partial(self.project_out, t)
        steps["scatter"] = self.scatter
        steps["gather"] = self.gather
        steps["collect"] = self.collect
        return steps

    def finish(self):
        for end in self.ends:
            end()


def kernel(gather, layer, *refs):
    lengths, hidden, gain, q, k, v = refs[:6]
    sources, (held, mixed) = refs[6:12], refs[12:14]
    moved, ring, late, small, sent, got, own, hidden_here, gain_here, lengths_here = refs[14:24]
    gather.begin(held, moved, ring, late, sent, got)
    gather.greet()
    high, low = q.shape[0], k.shape[0]
    pairs = [
        (q, moved.at[0, pl.ds(0, high), :]),
        (k, small.at[0]),
        (v, small.at[1]),
        (hidden, hidden_here),
        (gain, gain_here),
        (lengths, lengths_here),
    ]
    loads = [pltpu.make_async_copy(a, b, own.at[i]) for i, (a, b) in enumerate(pairs)]
    for load in loads:
        load.start()
    layer.begin(hidden_here, lengths_here, gain_here, sources, mixed, refs[24:])
    gather.meet(loads)
    moved[0, pl.ds(high, 2 * low), :] = jnp.concatenate([small[0], small[1]], axis=0)
    steps = [*gather.steps().values(), *layer.steps().values()]
    for number in ORDER:
        steps[number]()
    gather.finish()
    layer.finish()


def write_out(held, mixed, q, k, v, out, low_k, low_v, sems):
    high, low = q.shape[3], k.shape[2] // 4
    copies = [pltpu.make_async_copy(held.at[:, :, :, pl.ds(0, high), :], q, sems.at[0])]
    copies[0].start()
    for core in range(2):
        for slot in range(2):
            for at, (staged, target) in enumerate(((low_k, k), (low_v, v))):
                rows = slice(high + at * low, high + (at + 1) * low)
                staged[core, slot] = jnp.concatenate([held[core, slot, x, rows, :] for x in range(4)], axis=0)
                part = (core, slot)
                copies.append(pltpu.make_async_copy(staged.at[part], target.at[part], sems.at[len(copies)]))
                copies[-1].start()
    steps, rows, _ = out.shape
    share = mixed.shape[2]
    for t in range(mixed.shape[0]):
        for s in range(steps):
            out[s, :, t * share : (t + 1) * share] = mixed[t, s * rows : (s + 1) * rows, :].astype(BF)
    for copy in copies:
        copy.wait()


def on_device(
    hidden,
    lengths,
    norm_gain,
    w_query,
    key_weight_matrix,
    value_weight_matrix,
    w_out,
    key_cache,
    cached_value_rows,
    next_query,
    upcoming_key_weight,
    upcoming_value_weight,
):
    step_count, row_count, width = hidden.shape
    head = key_cache.shape[3]
    group = w_query.shape[1] // head
    context = key_cache.shape[2]
    tokens = step_count * row_count
    high, low = next_query.shape[0], upcoming_key_weight.shape[0]
    rows = high + 2 * low
    gather = Gather(rows, width)
    layer = Layer(step_count, row_count, width, group, head, context)
    vmem = pl.BlockSpec(memory_space=pltpu.VMEM)
    hbm = pl.BlockSpec(memory_space=pltpu.HBM)
    held, mixed = pl.pallas_call(
        functools.partial(kernel, gather, layer),
        out_shape=(
            jax.ShapeDtypeStruct((2, 2, 4, rows, width), BF),
            jax.ShapeDtypeStruct((8, tokens, width // 8), F32),
        ),
        in_specs=[hbm] * 12,
        out_specs=(pl.BlockSpec(memory_space=pl.ANY),) * 2,
        scratch_shapes=[
            *gather.scratch()[:3],
            pltpu.VMEM((2, low, width), BF),
            *gather.scratch()[3:],
            pltpu.SemaphoreType.DMA((6,)),
            pltpu.VMEM((step_count, row_count, width), BF),
            pltpu.VMEM((1, width), F32),
            pltpu.SMEM((row_count,), jnp.int32),
            *layer.scratch(),
        ],
        compiler_params=pltpu.CompilerParams(
            collective_id=0, has_side_effects=True, vmem_limit_bytes=VMEM_LIMIT
        ),
        cost_estimate=pl.CostEstimate(flops=10**9, bytes_accessed=40 * 2**20, transcendentals=10**5),
    )(
        *(
            pltpu.with_memory_space_constraint(each, pltpu.HBM)
            for each in (
                lengths,
                hidden,
                norm_gain.reshape(1, width),
                next_query,
                upcoming_key_weight,
                upcoming_value_weight,
                w_query,
                key_weight_matrix,
                value_weight_matrix,
                w_out,
                key_cache,
                cached_value_rows,
            )
        ),
    )
    q, k, v, mixed = pl.pallas_call(
        write_out,
        out_shape=(
            jax.ShapeDtypeStruct((2, 2, 4, high, width), BF),
            jax.ShapeDtypeStruct((2, 2, 4 * low, width), BF),
            jax.ShapeDtypeStruct((2, 2, 4 * low, width), BF),
            jax.ShapeDtypeStruct((step_count, row_count, width), BF),
        ),
        in_specs=[vmem] * 2,
        out_specs=(hbm, hbm, hbm, vmem),
        scratch_shapes=[
            pltpu.VMEM((2, 2, 4 * low, width), BF),
            pltpu.VMEM((2, 2, 4 * low, width), BF),
            pltpu.SemaphoreType.DMA((9,)),
        ],
        compiler_params=pltpu.CompilerParams(vmem_limit_bytes=16 * 2**20),
    )(
        pltpu.with_memory_space_constraint(held, pltpu.VMEM),
        pltpu.with_memory_space_constraint(mixed, pltpu.VMEM),
    )
    return mixed, q.reshape(-1, width), k.reshape(-1, width), v.reshape(-1, width)


def solution(mesh):
    in_specs = (
        P(None, "dp", None),
        P("dp"),
        P(),
        P(None, "tp"),
        P(None, "tp"),
        P(None, "tp"),
        P("tp", None),
        P("dp", "tp", None, None),
        P("dp", "tp", None, None),
        P(("dp", "tp"), None),
        P(("dp", "tp"), None),
        P(("dp", "tp"), None),
    )
    out_specs = (P(None, "dp", None), P("tp", None), P("tp", None), P("tp", None))
    return jax.shard_map(
        on_device, mesh=mesh, in_specs=in_specs, out_specs=out_specs, check_vma=False
    )
```
